512 devices in a mesh: gossip: 16 (over x, y_lo, core), zero: 32 (over z, y_hi).
Axes of the slice: x: 4, y: 4 (y_hi: 2, y_lo: 2; y = y_hi * 2 + y_lo), z: 16, core: 2. Of those that a mesh axis runs over, the one named last changes fastest.
Arguments:
- queries: bfloat16 [512, 256, 2560], P(('gossip', 'zero')), may hold values from -6 to 6
- keys: bfloat16 [512, 256, 2560], P(('gossip', 'zero')), may hold values from -6 to 6
- values: bfloat16 [512, 256, 2560], P(('gossip', 'zero')), may hold values from -24 to 24
- pattern: int32 [512, 2, 3], P(('gossip', 'zero')), may hold values from 0 to 1, as said below
- out_weight: bfloat16 [2560, 2560], P(None, 'zero'), may hold values from -0.125 to 0.125
- adapt_a: float32 [16, 2560, 64], P('gossip', 'zero'), may hold values from -5 to 5
- adapt_b: float32 [16, 64, 2560], P('gossip', None, 'zero'), may hold values from -5 to 5
Outputs:
- new_a: float32 [16, 2560, 64], P('gossip', 'zero')
- new_b: float32 [16, 64, 2560], P('gossip', None, 'zero')
The draws below stay inside these ranges and needn't reach their ends.
Inputs may be any that keep to these rules, and one draw needn't show every extreme that they name: pattern[s, a, 0] is a; every entry of row a is at most a.
All inputs are finite; a program needn't handle non-finite values.
Results may differ from the reference program's by a relative error of at most 0.004.
Values may be sent and summed in bfloat16 or wider, within the bound.
A program may use at most 64 MiB of HBM per device.

```python
import math
import jax
import jax.numpy as jnp
from jax import lax

HEADS = 20
HEAD_SIZE = 128
HD = 2560
DW = 2560
RANK = 64
TILE = 128
KPER = 3
TOK_DEV = 256
DIST = 2
SEQS = 512
QT = 2
N_GOSSIP = 16
N_ZERO = 32


def draw_queries(key, part):
    key = jax.random.fold_in(key, 1)
    drawn = jnp.clip(jax.random.normal(key, (SEQS, TOK_DEV, HD), jnp.float32), -6.0, 6.0)
    return drawn.astype(jnp.bfloat16)


def draw_keys(key, part):
    key = jax.random.fold_in(key, 2)
    drawn = jnp.clip(jax.random.normal(key, (SEQS, TOK_DEV, HD), jnp.float32), -6.0, 6.0)
    return drawn.astype(jnp.bfloat16)


def draw_pattern(key, part):
    key = jax.random.fold_in(key, 5)
    tile_count = TOK_DEV // TILE
    tile_rows = jnp.arange(tile_count, dtype=jnp.int32)[None, :, None]
    picks = jax.random.randint(key, (SEQS, tile_count, KPER), 0, 1 << 20) % (tile_rows + 1)
    column = jnp.arange(KPER, dtype=jnp.int32)[None, None, :]
    return jnp.where(column == 0, tile_rows, picks).astype(jnp.int32)


def strengthened(drawn, key, source, target, blocks, factor):
    def block_of(position):
        return (jnp.arange(drawn.shape[position]) // (drawn.shape[position] // blocks)).reshape((-1,) + (1,) * (drawn.ndim - 1 - position))

    one_side = jax.random.permutation(key, blocks)[block_of(target)]
    far = (block_of(target) + blocks // 2) % blocks
    return jnp.where((block_of(source) == one_side) | (block_of(source) == far), factor * drawn, drawn)


def shard_levels(own_key, extent, shards, low, high):
    def one(dim, blocks):
        draws = jax.random.uniform(jax.random.fold_in(jax.random.fold_in(own_key, 6), dim), (blocks,), jnp.float32, low / len(shards), high / len(shards))
        return jnp.repeat(jnp.exp(draws), extent[dim] // blocks).reshape((-1,) + (1,) * (len(extent) - dim - 1))

    loudness = one(*shards[0])
    for cut in shards[1:]:
        loudness = loudness * one(*cut)
    return loudness


def normal_values(rng, dims, scale, limit, cuts=(), kind=jnp.bfloat16):
    result = scale * jax.random.normal(rng, dims, jnp.float32)
    if cuts:
        result = result * shard_levels(rng, dims, cuts, -0.22, 0.18)
    return jnp.clip(result, -limit, limit).astype(kind)


def bell_draw_with(own_key, dims, scale, reach, pieces, heavy, kind=jnp.bfloat16):
    drawn = scale * jax.random.normal(own_key, dims, jnp.float32)
    if pieces:
        drawn = drawn * shard_levels(own_key, dims, pieces, -0.22, 0.18)
    return jnp.clip(strengthened(drawn, jax.random.fold_in(own_key, 3), *heavy), -reach, reach).astype(kind)


def setup_inputs(seed: int = 0) -> dict:
    arg_keys = jax.random.split(jax.random.key(seed), 8)
    return {
        "queries": draw_queries(jax.random.fold_in(arg_keys[7], 71), 0),
        "keys": draw_keys(jax.random.fold_in(arg_keys[7], 71), 0),
        "values": bell_draw_with(arg_keys[2], (SEQS, TOK_DEV, HD), 1.0, 24.0, ((0, 512),), (0, 2, 512, 6.0)),
        "pattern": draw_pattern(jax.random.fold_in(arg_keys[7], 71), 0),
        "out_weight": normal_values(arg_keys[4], (HD, DW), HD ** -0.5, 0.125, ((1, 32),)),
        "adapt_a": normal_values(arg_keys[5], (N_GOSSIP, HD, RANK), 1.0, 5.0, ((0, 16), (1, 32)), jnp.float32),
        "adapt_b": normal_values(arg_keys[6], (N_GOSSIP, RANK, DW), 1.0, 5.0, ((0, 16), (2, 32)), jnp.float32),
    }


step_rate = 0.5
sharpness = 4.0

def tile_mask(pattern, tile_size):
    count = pattern.shape[1]
    same = pattern[:, :, None] == pattern[:, None, :]
    earlier = jnp.arange(count)[None, :] < jnp.arange(count)[:, None]
    repeated = jnp.any(same & earlier[None], axis=2)
    tile_rows = jnp.arange(pattern.shape[0], dtype=jnp.int32)[:, None]
    before = (pattern < tile_rows) & ~repeated
    diagonal = (pattern == tile_rows) & ~repeated
    positions = jnp.arange(tile_size)
    causal = positions[None, :] <= positions[:, None]
    allowed = before[:, None, :, None] | diagonal[:, None, :, None] & causal[None, :, None, :]
    return allowed

def attend(queries, keys, values, pattern):
    tile_count = pattern.shape[0]
    per_row = pattern.shape[1]
    tile_size = queries.shape[0] // tile_count
    query_tiles = queries.reshape(tile_count, tile_size, HEADS, HEAD_SIZE).astype(jnp.float32)
    key_tiles = keys.reshape(tile_count, tile_size, HEADS, HEAD_SIZE)
    value_tiles = values.reshape(tile_count, tile_size, HEADS, HEAD_SIZE)
    flat_index = pattern.reshape(-1).astype(jnp.int32)
    key_chosen = jnp.take(key_tiles, flat_index, axis=0).reshape(tile_count, per_row, tile_size, HEADS, HEAD_SIZE)
    value_chosen = jnp.take(value_tiles, flat_index, axis=0).reshape(tile_count, per_row, tile_size, HEADS, HEAD_SIZE)
    scores = jnp.einsum('aqhd,ajkhd->ahqjk', query_tiles, key_chosen.astype(jnp.float32)) / math.sqrt(HEAD_SIZE)
    allowed = tile_mask(pattern, tile_size)[:, None]
    scores = jnp.where(allowed, scores, jnp.float32(-1e+30))
    highest = lax.optimization_barrier(jnp.max(scores, axis=(3, 4), keepdims=True))
    weights = jnp.where(allowed, jnp.exp(scores - highest), jnp.float32(0.0))
    totals = lax.optimization_barrier(jnp.sum(weights, axis=(3, 4), keepdims=True))
    probs = (weights / totals).astype(jnp.bfloat16)
    context = jnp.einsum('ahqjk,ajkhd->aqhd', probs.astype(jnp.float32), value_chosen.astype(jnp.float32))
    return context.astype(jnp.bfloat16).reshape(tile_count * tile_size, HEADS * HEAD_SIZE)

def one_sequence(out_weight, a_half, b_half, queries, keys, values, pattern):
    scale_adapt = 1.0 / math.sqrt(HD * RANK)
    context = attend(queries, keys, values, pattern)
    adapter_low = jnp.dot(context, a_half, preferred_element_type=jnp.float32).astype(jnp.bfloat16)
    output = jnp.dot(context, out_weight, preferred_element_type=jnp.float32) + scale_adapt * jnp.dot(adapter_low, b_half, preferred_element_type=jnp.float32)
    grad_out = jnp.tanh(sharpness * output).astype(jnp.bfloat16)
    hidden_grad = jnp.dot(grad_out, b_half.T, preferred_element_type=jnp.float32).astype(jnp.bfloat16)
    grad_a = scale_adapt * jnp.dot(context.T, hidden_grad, preferred_element_type=jnp.float32)
    grad_b = scale_adapt * jnp.dot(adapter_low.T, grad_out, preferred_element_type=jnp.float32)
    return (grad_a, grad_b)

def reference(queries, keys, values, pattern, out_weight, adapt_a, adapt_b):
    group_count = N_GOSSIP
    members = N_ZERO
    group_q = queries.reshape(group_count, members, TOK_DEV, HD)
    group_k = keys.reshape(group_count, members, TOK_DEV, HD)
    group_v = values.reshape(group_count, members, TOK_DEV, HD)
    group_p = pattern.reshape(group_count, members, QT, KPER)

    def one_group(items):
        own_a, own_b, seq_q, seq_k, seq_v, seq_p = items
        a_half = own_a.astype(jnp.bfloat16)
        b_half = own_b.astype(jnp.bfloat16)

        def add_sequence(carry, member):
            sum_a, sum_b = carry
            grad_a, grad_b = one_sequence(out_weight, a_half, b_half, member[0], member[1], member[2], member[3])
            return ((sum_a + grad_a, sum_b + grad_b), None)
        start = (jnp.zeros((HD, RANK), jnp.float32), jnp.zeros((RANK, DW), jnp.float32))
        (sum_a, sum_b), _ = lax.scan(add_sequence, start, (seq_q, seq_k, seq_v, seq_p))
        return (own_a - step_rate * sum_a, own_b - step_rate * sum_b)
    moved_a, moved_b = lax.map(one_group, (adapt_a, adapt_b, group_q, group_k, group_v, group_p))
    new_a = 0.5 * (moved_a + jnp.roll(moved_a, DIST, axis=0))
    new_b = 0.5 * (moved_b + jnp.roll(moved_b, DIST, axis=0))
    return (new_a, new_b)
```

```python
import functools
import math

import jax
import jax.numpy as jnp
from jax import lax
from jax.experimental import pallas as pl
from jax.experimental.pallas import tpu as pltpu
from jax.sharding import PartitionSpec as P

MESH = pl.DeviceIdType.MESH
HEAD = 128
TILE = 128
DIST = 2
RING = 4
STEP_RATE = 0.5
SHARPNESS = 4.0
F32 = jnp.float32
BF16 = jnp.bfloat16


def nn(a, b):
    return lax.dot_general(a, b, (((1,), (0,)), ((), ())), preferred_element_type=F32)


def nt(a, b):
    return lax.dot_general(a, b, (((1,), (1,)), ((), ())), preferred_element_type=F32)


def tn(a, b):
    return lax.dot_general(a, b, (((0,), (0,)), ((), ())), preferred_element_type=F32)


def kernel(
    nz, n_gossip, hd, rank,
    q_hbm, k_hbm, v_hbm, pattern, w_hbm, a_ref, b_ref,
    out_a, out_b,
    q, k, v, wt, ab, abf, square, mask0, mask1, ctx, low, low_t, hid, gb, grads, summed, theirs, landed, moved, partner,
    load_sem, opp_sem, zu_send, zu_recv, zd_send, zd_recv,
    right_send, left_send, left_recv, right_recv, on_send, on_recv, sib_send, sib_recv,
    abp_sem, abu_send, abu_recv, abd_send, abd_recv,
    yx_send, yx_recv, own_send, own_recv, gos_sem,
):
    half = nz // 2
    width = hd // 4
    rows = hd // (2 * nz)
    heads = hd // HEAD
    scale = 1.0 / math.sqrt(hd * rank)

    gossip, zero = lax.axis_index("gossip"), lax.axis_index("zero")
    core = lax.rem(gossip, 2)
    y_lo = lax.rem(lax.div(gossip, 2), 2)
    x = lax.div(gossip, 4)
    z = lax.div(zero, 2)
    y_hi = lax.rem(zero, 2)
    y = y_hi * 2 + y_lo
    place = core * y + (1 - core) * x

    def spread_device(step):
        xs = lax.rem(x + step + RING, RING)
        ys = lax.rem(y + step + RING, RING)
        g0, z0 = (xs * 2 + y_lo) * 2, zero
        g1, z1 = (x * 2 + lax.rem(ys, 2)) * 2 + 1, z * 2 + lax.div(ys, 2)
        return core * g1 + (1 - core) * g0, core * z1 + (1 - core) * z0

    def z_device(step):
        return gossip, lax.rem(z + step + nz, nz) * 2 + y_hi

    opposite = ((x * 2 + 1 - y_lo) * 2 + core, z * 2 + 1 - y_hi)
    sibling = ((x * 2 + y_lo) * 2 + 1 - core, zero)
    mate = (gossip, z * 2 + 1 - y_hi)
    right, left = spread_device(1), spread_device(-1)
    after = (lax.rem(gossip + DIST, n_gossip), zero)
    before = (lax.rem(gossip + n_gossip - DIST, n_gossip), zero)

    barrier = pltpu.get_barrier_semaphore()

    def greet(device):
        pl.semaphore_signal(barrier, inc=1, device_id=device, device_id_type=MESH)

    for device in (right, left, opposite, sibling, mate, after, before):
        greet(device)

    @pl.loop(1, nz)
    def _(i):
        greet(z_device(i))

    def block(step):
        p = lax.rem(place + step + RING, RING)
        return core * 2 + lax.rem(p, 2), lax.div(p, 2)

    kb, r = block(0)
    crosses = (r == y_hi) & (core == 0)

    def plane(i):
        s, odd = lax.div(i + 1, 2), lax.rem(i, 2)
        return lax.rem(z + nz + s - 2 * odd * s, nz)

    def copy(src, dst, send, recv, device):
        return pltpu.make_async_remote_copy(
            src_ref=src, dst_ref=dst, send_sem=send, recv_sem=recv, device_id=device, device_id_type=MESH
        )

    loads = [
        pltpu.make_async_copy(q_hbm.at[0], q, load_sem.at[1]),
        pltpu.make_async_copy(k_hbm.at[0], k, load_sem.at[2]),
        pltpu.make_async_copy(v_hbm.at[0], v, load_sem.at[3]),
    ]
    own = pltpu.make_async_copy(
        w_hbm.at[:, pl.ds(pl.multiple_of(kb * width, 128), width)], wt.at[kb, z, r], load_sem.at[0]
    )

    @pl.when(r == y_hi)
    def _():
        own.start()

    for load in loads:
        load.start()

    square[...] = jnp.zeros_like(square)
    square[0:rank, 0:rows] = a_ref[0]
    square[rank:, 0:rows] = b_ref[0]
    abf[...] = square[...].T[0:rows]
    ab[z, y_hi] = abf[...].astype(BF16)

    key_at = lax.broadcasted_iota(jnp.int32, (TILE, 2 * TILE), 0)
    query_at = lax.broadcasted_iota(jnp.int32, (TILE, 2 * TILE), 1)
    sees = (pattern[0, 1, 1] == 0) | (pattern[0, 1, 2] == 0)
    far = jnp.where(sees, F32(0.0), F32(-1e30))
    mask0[...] = jnp.where(query_at < TILE, jnp.where(key_at <= query_at, F32(0.0), F32(-1e30)), far)
    mask1[...] = jnp.where(key_at <= query_at, F32(0.0), F32(-1e30))[:, 0:TILE]

    @pl.when(r == y_hi)
    def _():
        own.wait()

    pl.semaphore_wait(barrier, nz - 1 + 7)

    def cross():
        return copy(wt.at[kb, z, r], wt.at[kb, z, r], opp_sem.at[0], opp_sem.at[1], opposite)

    def up(s):
        at = wt.at[kb, lax.rem(z - s + nz, nz), r]
        return copy(at, at, zu_send.at[s], zu_recv.at[s + 1], z_device(1))

    def up_in(s):
        at = wt.at[kb, lax.rem(z - s + nz, nz), r]
        return copy(at, at, zu_send.at[s], zu_recv.at[s], z_device(1))

    def down(s):
        at = wt.at[kb, lax.rem(z + s, nz), r]
        return copy(at, at, zd_send.at[s], zd_recv.at[s + 1], z_device(-1))

    def down_in(s):
        at = wt.at[kb, lax.rem(z + s, nz), r]
        return copy(at, at, zd_send.at[s], zd_recv.at[s], z_device(-1))

    def to_right(i):
        at = wt.at[kb, plane(i), r]
        return copy(at, at, right_send.at[i], left_recv.at[i], right)

    def to_left(i):
        at = wt.at[kb, plane(i), r]
        return copy(at, at, left_send.at[i], right_recv.at[i], left)

    def from_left(i):
        n, m = block(-1)
        at = wt.at[n, plane(i), m]
        return copy(at, at, on_send.at[i], left_recv.at[i], right)

    def from_right(i):
        n, m = block(1)
        at = wt.at[n, plane(i), m]
        return copy(at, at, on_send.at[i], right_recv.at[i], left)

    def on_right(i):
        n, m = block(-1)
        at = wt.at[n, plane(i), m]
        return copy(at, at, on_send.at[i], on_recv.at[i], right)

    def on_left(i):
        n, m = block(1)
        at = wt.at[n, plane(i), m]
        return copy(at, at, on_send.at[i], on_recv.at[i], left)

    def on_in(i):
        n, m = block(2)
        at = wt.at[n, plane(i), m]
        return copy(at, at, on_send.at[i], on_recv.at[i], right)

    def across(i):
        at = wt.at[pl.ds(core * 2, 2), plane(i)]
        return copy(at, at, sib_send.at[i], sib_recv.at[i], sibling)

    def across_in(i):
        at = wt.at[pl.ds(2 - core * 2, 2), plane(i)]
        return copy(at, at, sib_send.at[i], sib_recv.at[i], sibling)

    def spread(i):
        to_right(i).start()
        to_left(i).start()

    def arrive(s):
        up_in(s).wait_recv()
        if s < half:
            up(s).start()
        spread(2 * s - 1)
        if s < half:
            down_in(s).wait_recv()
            if s < half - 1:
                down(s).start()
            spread(2 * s)

    def hand_on(s):
        i = max(2 * s - 1, 0)
        from_left(i).wait_recv()
        on_right(i).start()
        from_right(i).wait_recv()
        if 0 < s < half:
            from_right(2 * s).wait_recv()
            on_left(2 * s).start()
            from_left(2 * s).wait_recv()

    def share(s):
        on_in(max(2 * s - 1, 0)).wait_recv()
        across(max(2 * s - 1, 0)).start()
        if 0 < s < half:
            on_in(2 * s).wait_recv()
            across(2 * s).start()

    def ab_mate(which):
        at = ab.at[z, which]
        return copy(at, at, abp_sem.at[0], abp_sem.at[1], mate)

    def ab_up(s, slot):
        at = ab.at[lax.rem(z - s + nz, nz)]
        return copy(at, at, abu_send.at[s], abu_recv.at[slot], z_device(1))

    def ab_down(s, slot):
        at = ab.at[lax.rem(z + s, nz)]
        return copy(at, at, abd_send.at[s], abd_recv.at[slot], z_device(-1))

    def ab_step(s):
        ab_up(s, s).wait_recv()
        if s < half:
            ab_up(s, s + 1).start()
            ab_down(s, s).wait_recv()
            if s < half - 1:
                ab_down(s, s + 1).start()

    fold = F32(math.log2(math.e) / math.sqrt(HEAD))

    def attend(first, last):
        @pl.loop(first, last)
        def _(h):
            at = pl.ds(pl.multiple_of(h * HEAD, HEAD), HEAD)
            qh = q[:, at]
            s0 = nt(k[0:TILE, at], qh) * fold + mask0[...]
            s1 = nt(k[TILE:, at], qh[TILE:]) * fold + mask1[...]
            top0 = jnp.max(s0, axis=0, keepdims=True)
            top1 = jnp.max(s1, axis=0, keepdims=True)
            top1 = jnp.maximum(top0[:, TILE:], top1)
            e00 = jnp.exp2(s0[:, 0:TILE] - top0[:, 0:TILE])
            e01 = jnp.exp2(s0[:, TILE:] - top1)
            e11 = jnp.exp2(s1 - top1)
            total0 = jnp.sum(e00, axis=0, keepdims=True)
            total1 = jnp.sum(e01, axis=0, keepdims=True) + jnp.sum(e11, axis=0, keepdims=True)
            v0, v1 = v[0:TILE, at], v[TILE:, at]
            c0 = tn(v0, e00.astype(BF16)) / total0
            c1 = (tn(v0, e01.astype(BF16)) + tn(v1, e11.astype(BF16))) / total1
            ctx[at, 0:TILE] = c0.astype(BF16)
            ctx[at, TILE:] = c1.astype(BF16)

    def project(first, last):
        @pl.loop(first, last)
        def _(i):
            across_in(i).wait_recv()
            w = plane(i)
            factors = ab[w].reshape(2 * rows, 2 * rank)
            out = scale * nn(factors, low[...])
            for n in range(4):
                out += nn(wt[n, w].reshape(2 * rows, width), ctx[n * width : (n + 1) * width])
            slope = jnp.tanh(SHARPNESS * out).astype(BF16)
            hid[...] += tn(factors, slope)
            gb[w] = nn(slope, low_t[...])

    @pl.when(crosses)
    def _():
        cross().start()

    ab_mate(y_hi).start()

    @pl.when(r != y_hi)
    def _():
        cross().wait_recv()

    up(0).start()
    down(0).start()
    spread(0)
    for load in loads:
        load.wait()
    hid[...] = jnp.zeros_like(hid)
    cut = [heads * n // 4 for n in range(5)]
    ab_mate(1 - y_hi).wait_recv()
    ab_up(0, 1).start()
    ab_down(0, 1).start()

    def ab_steps(first, last):
        for s in range(first, last):
            if s <= half:
                ab_step(s)

    attend(cut[0], cut[1])
    ab_steps(1, 2)
    arrive(1)
    hand_on(0)
    attend(cut[1], cut[2])
    ab_steps(2, 3)
    share(0)
    attend(cut[2], cut[3])
    ab_steps(3, 4)
    if half >= 2:
        arrive(2)
    hand_on(1)
    attend(cut[3], cut[4])
    ab_steps(4, 6)
    share(1)
    if half >= 3:
        arrive(3)
    if half >= 2:
        hand_on(2)
        share(2)
    ab_steps(6, 9)

    both = tn(ab[...].reshape(hd, 2 * rank), ctx[...])
    low[0:rank] = jnp.zeros((rank, 2 * TILE), BF16)
    low[rank:] = both[0:rank].astype(BF16)
    low_t[...] = low[...].astype(F32).T.astype(BF16)

    done = 0

    def project_to(s):
        nonlocal done
        last = min(2 * s + 1, nz)
        if last > done:
            project(done, last)
            done = last

    for s in range(4, half + 1):
        arrive(s)
        project_to(2 * (s - 4) + (s > 4) if s < 6 else s - 2)
        hand_on(s - 1)
        share(s - 1)
    if half >= 3:
        project_to(half - 1)
        hand_on(half)
        share(half)
    project_to(half)

    square[...] = jnp.zeros_like(square)
    hid_t = jnp.concatenate([hid[rank:], jnp.zeros((rank, 2 * TILE), F32)], axis=0).T.astype(BF16)

    def trade(i):
        w = plane(i)
        return copy(grads.at[w, 1 - y_hi], theirs.at[w], yx_send.at[i], yx_recv.at[i], mate)

    def give(i):
        w = plane(i)
        return copy(summed.at[w], landed.at[z], own_send.at[i], own_recv.at[z], (gossip, w * 2 + y_hi))

    def take(i):
        w = plane(i)
        return copy(summed.at[w], landed.at[w], own_send.at[i], own_recv.at[w], (gossip, w * 2 + y_hi))

    @pl.loop(0, nz)
    def _(n):
        i = nz - 1 - n
        w = plane(i)
        part = ctx[pl.ds(pl.multiple_of(w * 2 * rows, 2 * rows), 2 * rows)]
        both = scale * (nn(part, hid_t) + gb[w])
        grads[w] = both.astype(BF16).reshape(2, rows, 2 * rank)
        trade(i).start()

    @pl.loop(0, nz - 1)
    def _(n):
        i = nz - 1 - n
        w = plane(i)
        trade(i).wait_recv()
        summed[w] = (grads[w, y_hi].astype(F32) + theirs[w].astype(F32)).astype(BF16)
        give(i).start()

    trade(0).wait_recv()
    moved[...] = grads[z, y_hi].astype(F32) + theirs[z].astype(F32)

    @pl.loop(1, nz)
    def _(i):
        take(i).wait_recv()
        moved[...] += landed[plane(i)].astype(F32)

    moved[...] = abf[...] - STEP_RATE * moved[...]
    gossip_copy = copy(moved, partner, gos_sem.at[0], gos_sem.at[1], after)
    gossip_copy.start()
    gossip_copy.wait_recv()
    new = 0.5 * (moved[...] + partner[...])
    square[0:rows] = new
    turned = square[...].T
    out_a[0] = turned[0:rank, 0:rows]
    out_b[0] = turned[rank:, 0:rows]

    gossip_copy.wait_send()

    @pl.when(crosses)
    def _():
        cross().wait_send()

    ab_mate(y_hi).wait_send()

    @pl.loop(0, half)
    def _(s):
        up(s).wait_send()
        ab_up(s, s + 1).wait_send()

    @pl.loop(0, half - 1)
    def _(s):
        down(s).wait_send()
        ab_down(s, s + 1).wait_send()

    @pl.loop(0, nz)
    def _(i):
        to_right(i).wait_send()
        to_left(i).wait_send()
        on_in(i).wait_send()
        across(i).wait_send()
        trade(i).wait_send()

    @pl.loop(1, nz)
    def _(i):
        give(i).wait_send()


def solution(mesh):
    n_gossip, n_zero = mesh.shape["gossip"], mesh.shape["zero"]
    nz = n_zero // 2
    half = nz // 2

    def per_device(queries, keys, values, pattern, out_weight, adapt_a, adapt_b):
        _, tokens, hd = queries.shape
        rows, rank = adapt_a.shape[1:]
        width = hd // 4
        dma = pltpu.SemaphoreType.DMA
        vmem = pltpu.VMEM
        whole = pl.BlockSpec(memory_space=pltpu.VMEM)
        place = pl.BlockSpec(memory_space=pl.ANY)
        flops = 2 * tokens * hd * (hd + 2 * tokens + 4 * rank)
        new_a, new_b = pl.pallas_call(
            functools.partial(kernel, nz, n_gossip, hd, rank),
            out_shape=(
                jax.ShapeDtypeStruct((1, rank, rows), F32),
                jax.ShapeDtypeStruct((1, rank, rows), F32),
            ),
            in_specs=[place, place, place, pl.BlockSpec(memory_space=pltpu.SMEM), place, whole, whole],
            out_specs=(whole, whole),
            scratch_shapes=[
                vmem((tokens, hd), BF16), vmem((tokens, hd), BF16), vmem((tokens, hd), BF16),
                vmem((4, nz, 2, rows, width), BF16),
                vmem((nz, 2, rows, 2 * rank), BF16), vmem((rows, 2 * rank), F32), vmem((2 * rank, 128), F32),
                vmem((TILE, 2 * TILE), F32), vmem((TILE, TILE), F32),
                vmem((hd, tokens), BF16), vmem((2 * rank, tokens), BF16), vmem((tokens, 2 * rank), BF16),
                vmem((2 * rank, tokens), F32), vmem((nz, 2 * rows, 2 * rank), F32),
                vmem((nz, 2, rows, 2 * rank), BF16), vmem((nz, rows, 2 * rank), BF16),
                vmem((nz, rows, 2 * rank), BF16), vmem((nz, rows, 2 * rank), BF16),
                vmem((rows, 2 * rank), F32), vmem((rows, 2 * rank), F32),
                dma((4,)), dma((2,)),
                dma((half + 1,)), dma((half + 1,)), dma((half + 1,)), dma((half + 1,)),
                dma((nz,)), dma((nz,)), dma((nz,)), dma((nz,)), dma((nz,)), dma((nz,)), dma((nz,)), dma((nz,)),
                dma((2,)), dma((half + 1,)), dma((half + 1,)), dma((half + 1,)), dma((half + 1,)),
                dma((nz,)), dma((nz,)), dma((nz,)), dma((nz,)), dma((2,)),
            ],
            compiler_params=pltpu.CompilerParams(
                collective_id=0, has_side_effects=True, vmem_limit_bytes=60 * 1024 * 1024
            ),
            cost_estimate=pl.CostEstimate(flops=flops, bytes_accessed=8 * tokens * hd, transcendentals=tokens * hd),
        )(queries, keys, values, pattern, out_weight.T, adapt_a.transpose(0, 2, 1), adapt_b)
        return new_a.transpose(0, 2, 1), new_b

    placed = (
        P(("gossip", "zero"), None, None),
        P(("gossip", "zero"), None, None),
        P(("gossip", "zero"), None, None),
        P(("gossip", "zero"), None, None),
        P(None, "zero"),
        P("gossip", "zero", None),
        P("gossip", None, "zero"),
    )
    return jax.shard_map(
        per_device,
        mesh=mesh,
        in_specs=placed,
        out_specs=(P("gossip", "zero", None), P("gossip", None, "zero")),
        check_vma=False,
    )
```

```python
import functools
import itertools
import math

import jax
import jax.numpy as jnp
from jax import lax
from jax.experimental import pallas as pl
from jax.experimental.pallas import tpu as pltpu
from jax.sharding import PartitionSpec as P

MESH = pl.DeviceIdType.MESH
HEAD = 128
TILE = 128
DIST = 2
RING = 4
STEP_RATE = 0.5
SHARPNESS = 4.0
F32 = jnp.float32
BF16 = jnp.bfloat16


def nn(a, b):
    return lax.dot_general(a, b, (((1,), (0,)), ((), ())), preferred_element_type=F32)


def nt(a, b):
    return lax.dot_general(a, b, (((1,), (1,)), ((), ())), preferred_element_type=F32)


def tn(a, b):
    return lax.dot_general(a, b, (((0,), (0,)), ((), ())), preferred_element_type=F32)


def kernel(
    nz, n_gossip, hd, rank,
    q_hbm, k_hbm, v_hbm, pattern, w_hbm, a_ref, b_ref,
    out_a, out_b,
    q, k, v, wt, ab, abf, square, mask0, mask1, ctx, low, low_t, hid, gb, grads, summed, theirs, landed, moved, partner,
    load_sem, opp_sem, zu_send, zu_recv, zd_send, zd_recv,
    right_send, left_send, left_recv, right_recv, on_send, on_recv, sib_send, sib_recv,
    abp_sem, abu_send, abu_recv, abd_send, abd_recv,
    yx_send, yx_recv, own_send, own_recv, gos_sem,
):
    half = nz // 2
    jump = half // 2 if half >= 4 else 0
    firsts = (1, jump) if jump else (1,)
    width = hd // 4
    rows = hd // (2 * nz)
    heads = hd // HEAD
    scale = 1.0 / math.sqrt(hd * rank)

    gossip, zero = lax.axis_index("gossip"), lax.axis_index("zero")
    core = lax.rem(gossip, 2)
    y_lo = lax.rem(lax.div(gossip, 2), 2)
    x = lax.div(gossip, 4)
    z = lax.div(zero, 2)
    y_hi = lax.rem(zero, 2)
    y = y_hi * 2 + y_lo
    place = core * y + (1 - core) * x

    def spread_device(step):
        xs = lax.rem(x + step + RING, RING)
        ys = lax.rem(y + step + RING, RING)
        g0, z0 = (xs * 2 + y_lo) * 2, zero
        g1, z1 = (x * 2 + lax.rem(ys, 2)) * 2 + 1, z * 2 + lax.div(ys, 2)
        return core * g1 + (1 - core) * g0, core * z1 + (1 - core) * z0

    def z_device(step):
        return gossip, lax.rem(z + step + nz, nz) * 2 + y_hi

    opposite = ((x * 2 + 1 - y_lo) * 2 + core, z * 2 + 1 - y_hi)
    sibling = ((x * 2 + y_lo) * 2 + 1 - core, zero)
    mate = (gossip, z * 2 + 1 - y_hi)
    right, left = spread_device(1), spread_device(-1)
    after = (lax.rem(gossip + DIST, n_gossip), zero)
    before = (lax.rem(gossip + n_gossip - DIST, n_gossip), zero)

    barrier = pltpu.get_barrier_semaphore()

    def greet(device):
        pl.semaphore_signal(barrier, inc=1, device_id=device, device_id_type=MESH)

    partners = [right, left, opposite, sibling, mate, after, before]
    for s in firsts:
        partners += [z_device(s), z_device(-s)] if 2 * s != nz else [z_device(s)]
    for device in partners:
        greet(device)

    def block(step):
        p = lax.rem(place + step + RING, RING)
        return core * 2 + lax.rem(p, 2), lax.div(p, 2)

    kb, r = block(0)
    crosses = (r == y_hi) & (core == 0)

    def plane(i):
        s, odd = lax.div(i + 1, 2), lax.rem(i, 2)
        return lax.rem(z + nz + s - 2 * odd * s, nz)

    def copy(src, dst, send, recv, device):
        return pltpu.make_async_remote_copy(
            src_ref=src, dst_ref=dst, send_sem=send, recv_sem=recv, device_id=device, device_id_type=MESH
        )

    loads = [
        pltpu.make_async_copy(q_hbm.at[0], q, load_sem.at[1]),
        pltpu.make_async_copy(k_hbm.at[0], k, load_sem.at[2]),
        pltpu.make_async_copy(v_hbm.at[0], v, load_sem.at[3]),
    ]
    own = pltpu.make_async_copy(
        w_hbm.at[:, pl.ds(pl.multiple_of(kb * width, 128), width)], wt.at[kb, z, r], load_sem.at[0]
    )

    @pl.when(r == y_hi)
    def _():
        own.start()

    for load in loads:
        load.start()

    square[...] = jnp.zeros_like(square)
    square[0:rank, 0:rows] = a_ref[0]
    square[rank:, 0:rows] = b_ref[0]
    abf[...] = square[...].T[0:rows]
    ab[z, y_hi] = abf[...].astype(BF16)

    key_at = lax.broadcasted_iota(jnp.int32, (TILE, 2 * TILE), 0)
    query_at = lax.broadcasted_iota(jnp.int32, (TILE, 2 * TILE), 1)
    sees = (pattern[0, 1, 1] == 0) | (pattern[0, 1, 2] == 0)
    far = jnp.where(sees, F32(0.0), F32(-1e30))
    mask0[...] = jnp.where(query_at < TILE, jnp.where(key_at <= query_at, F32(0.0), F32(-1e30)), far)
    mask1[...] = jnp.where(key_at <= query_at, F32(0.0), F32(-1e30))[:, 0:TILE]

    @pl.when(r == y_hi)
    def _():
        own.wait()

    pl.semaphore_wait(barrier, len(partners))

    def cross():
        return copy(wt.at[kb, z, r], wt.at[kb, z, r], opp_sem.at[0], opp_sem.at[1], opposite)

    def up(s, step=1):
        at = wt.at[kb, lax.rem(z - s + nz, nz), r]
        return copy(at, at, zu_send.at[s + step], zu_recv.at[s + step], z_device(step))

    def up_in(s):
        at = wt.at[kb, lax.rem(z - s + nz, nz), r]
        return copy(at, at, zu_send.at[s], zu_recv.at[s], z_device(1))

    def down(s, step=1):
        at = wt.at[kb, lax.rem(z + s, nz), r]
        return copy(at, at, zd_send.at[s + step], zd_recv.at[s + step], z_device(-step))

    def down_in(s):
        at = wt.at[kb, lax.rem(z + s, nz), r]
        return copy(at, at, zd_send.at[s], zd_recv.at[s], z_device(-1))

    def to_right(i):
        at = wt.at[kb, plane(i), r]
        return copy(at, at, right_send.at[i], left_recv.at[i], right)

    def to_left(i):
        at = wt.at[kb, plane(i), r]
        return copy(at, at, left_send.at[i], right_recv.at[i], left)

    def from_left(i):
        n, m = block(-1)
        at = wt.at[n, plane(i), m]
        return copy(at, at, on_send.at[i], left_recv.at[i], right)

    def from_right(i):
        n, m = block(1)
        at = wt.at[n, plane(i), m]
        return copy(at, at, on_send.at[i], right_recv.at[i], left)

    def on_right(i):
        n, m = block(-1)
        at = wt.at[n, plane(i), m]
        return copy(at, at, on_send.at[i], on_recv.at[i], right)

    def on_left(i):
        n, m = block(1)
        at = wt.at[n, plane(i), m]
        return copy(at, at, on_send.at[i], on_recv.at[i], left)

    def on_in(i):
        n, m = block(2)
        at = wt.at[n, plane(i), m]
        return copy(at, at, on_send.at[i], on_recv.at[i], right)

    def across(i):
        at = wt.at[pl.ds(core * 2, 2), plane(i)]
        return copy(at, at, sib_send.at[i], sib_recv.at[i], sibling)

    def across_in(i):
        at = wt.at[pl.ds(2 - core * 2, 2), plane(i)]
        return copy(at, at, sib_send.at[i], sib_recv.at[i], sibling)

    def spread(i):
        to_right(i).start()
        to_left(i).start()

    def arrive(s):
        up_in(s).wait_recv()
        if s < half and s + 1 not in firsts:
            up(s).start()
        spread(2 * s - 1)
        if s < half:
            down_in(s).wait_recv()
            if s < half - 1 and s + 1 not in firsts:
                down(s).start()
            spread(2 * s)

    def hand_on(s):
        i = max(2 * s - 1, 0)
        from_left(i).wait_recv()
        on_right(i).start()
        from_right(i).wait_recv()
        if 0 < s < half:
            from_right(2 * s).wait_recv()
            on_left(2 * s).start()
            from_left(2 * s).wait_recv()

    def share(s):
        on_in(max(2 * s - 1, 0)).wait_recv()
        across(max(2 * s - 1, 0)).start()
        if 0 < s < half:
            on_in(2 * s).wait_recv()
            across(2 * s).start()

    def ab_mate(which):
        at = ab.at[z, which]
        return copy(at, at, abp_sem.at[0], abp_sem.at[1], mate)

    def ab_up(s, step=1):
        at = ab.at[lax.rem(z - s + nz, nz)]
        return copy(at, at, abu_send.at[s + step], abu_recv.at[s + step], z_device(step))

    def ab_down(s, step=1):
        at = ab.at[lax.rem(z + s, nz)]
        return copy(at, at, abd_send.at[s + step], abd_recv.at[s + step], z_device(-step))

    def ab_in(s):
        at = ab.at[lax.rem(z - s + nz, nz)]
        copy(at, at, abu_send.at[s], abu_recv.at[s], z_device(1)).wait_recv()
        if s < half and s + 1 not in firsts:
            ab_up(s).start()
        if s < half:
            at = ab.at[lax.rem(z + s, nz)]
            copy(at, at, abd_send.at[s], abd_recv.at[s], z_device(-1)).wait_recv()
            if s < half - 1 and s + 1 not in firsts:
                ab_down(s).start()

    fold = F32(math.log2(math.e) / math.sqrt(HEAD))

    def attend(first, last):
        @pl.loop(first, last)
        def _(h):
            at = pl.ds(pl.multiple_of(h * HEAD, HEAD), HEAD)
            qh = q[:, at]
            s0 = nt(k[0:TILE, at], qh) * fold + mask0[...]
            s1 = nt(k[TILE:, at], qh[TILE:]) * fold + mask1[...]
            top0 = jnp.max(s0, axis=0, keepdims=True)
            top1 = jnp.max(s1, axis=0, keepdims=True)
            top1 = jnp.maximum(top0[:, TILE:], top1)
            e00 = jnp.exp2(s0[:, 0:TILE] - top0[:, 0:TILE])
            e01 = jnp.exp2(s0[:, TILE:] - top1)
            e11 = jnp.exp2(s1 - top1)
            total0 = jnp.sum(e00, axis=0, keepdims=True)
            total1 = jnp.sum(e01, axis=0, keepdims=True) + jnp.sum(e11, axis=0, keepdims=True)
            v0, v1 = v[0:TILE, at], v[TILE:, at]
            c0 = tn(v0, e00.astype(BF16)) / total0
            c1 = (tn(v0, e01.astype(BF16)) + tn(v1, e11.astype(BF16))) / total1
            ctx[at, 0:TILE] = c0.astype(BF16)
            ctx[at, TILE:] = c1.astype(BF16)

    def project(s):
        members = [max(2 * s - 1, 0)] + ([2 * s] if 0 < s < half else [])
        for i in members:
            across_in(i).wait_recv()
        planes = [plane(i) for i in members]

        def rows_of(blocks):
            return jnp.concatenate([b.reshape(2 * rows, b.shape[-1]) for b in blocks], axis=0)

        factors = rows_of([ab[w] for w in planes])
        out = scale * nn(factors, low[...])
        for n in range(4):
            out += nn(rows_of([wt[n, w] for w in planes]), ctx[n * width : (n + 1) * width])
        slope = jnp.tanh(SHARPNESS * out).astype(BF16)
        hid[...] += tn(factors, slope)
        second = nn(slope, low_t[...])
        for n, w in enumerate(planes):
            gb[w] = second[n * 2 * rows : (n + 1) * 2 * rows]

    @pl.when(crosses)
    def _():
        cross().start()

    ab_mate(y_hi).start()

    @pl.when(r != y_hi)
    def _():
        cross().wait_recv()

    for s in reversed(firsts):
        up(0, s).start()
        if s < half:
            down(0, s).start()
    spread(0)
    for load in loads:
        load.wait()
    hid[...] = jnp.zeros_like(hid)
    cut = [heads * n // 5 for n in range(6)]
    attend(cut[0], cut[1])
    ab_mate(1 - y_hi).wait_recv()
    for s in reversed(firsts):
        ab_up(0, s).start()
        if s < half:
            ab_down(0, s).start()
    attend(cut[1], cut[2])
    chains = [range(a, b) for a, b in zip(firsts, (*firsts[1:], half + 1))]
    ticks = [[s for s in tick if s is not None] for tick in itertools.zip_longest(*chains)]
    stages = [[0], *ticks]
    for n, tick in enumerate(ticks):
        for s in tick:
            arrive(s)
        for s in tick:
            ab_in(s)
        if n < 3:
            attend(cut[n + 2], cut[n + 3])
        for s in stages[n]:
            hand_on(s)
        for s in stages[n - 1] if n else ():
            share(s)
    for n in range(len(ticks), 3):
        attend(cut[n + 2], cut[n + 3])

    both = tn(ab[...].reshape(hd, 2 * rank), ctx[...])
    low[0:rank] = jnp.zeros((rank, 2 * TILE), BF16)
    low[rank:] = both[0:rank].astype(BF16)
    low_t[...] = low[...].astype(F32).T.astype(BF16)

    todo = [s for tick in stages[:-2] for s in tick]
    later = stages[-2]
    third = len(todo) // 3
    for s in todo[:third]:
        project(s)
    for s in stages[-1]:
        hand_on(s)
    for s in later:
        share(s)
    for s in todo[third : 2 * third]:
        project(s)
    for s in stages[-1]:
        share(s)
    for s in [*todo[2 * third :], *later, *stages[-1]]:
        project(s)

    square[...] = jnp.zeros_like(square)
    hid_t = jnp.concatenate([hid[rank:], jnp.zeros((rank, 2 * TILE), F32)], axis=0).T.astype(BF16)

    def trade(i):
        w = plane(i)
        return copy(grads.at[w, 1 - y_hi], theirs.at[w], yx_send.at[i], yx_recv.at[i], mate)

    def give(i):
        w = plane(i)
        return copy(summed.at[w], landed.at[z], own_send.at[i], own_recv.at[z], (gossip, w * 2 + y_hi))

    def take(i):
        w = plane(i)
        return copy(summed.at[w], landed.at[w], own_send.at[i], own_recv.at[w], (gossip, w * 2 + y_hi))

    @pl.loop(0, nz)
    def _(n):
        i = nz - 1 - n
        w = plane(i)
        part = ctx[pl.ds(pl.multiple_of(w * 2 * rows, 2 * rows), 2 * rows)]
        both = scale * (nn(part, hid_t) + gb[w])
        grads[w] = both.astype(BF16).reshape(2, rows, 2 * rank)
        trade(i).start()

    @pl.loop(0, nz - 1)
    def _(n):
        i = nz - 1 - n
        w = plane(i)
        trade(i).wait_recv()
        summed[w] = (grads[w, y_hi].astype(F32) + theirs[w].astype(F32)).astype(BF16)
        give(i).start()

    trade(0).wait_recv()
    moved[...] = grads[z, y_hi].astype(F32) + theirs[z].astype(F32)

    @pl.loop(1, nz)
    def _(i):
        take(i).wait_recv()
        moved[...] += landed[plane(i)].astype(F32)

    moved[...] = abf[...] - STEP_RATE * moved[...]
    gossip_copy = copy(moved, partner, gos_sem.at[0], gos_sem.at[1], after)
    gossip_copy.start()
    gossip_copy.wait_recv()
    new = 0.5 * (moved[...] + partner[...])
    square[0:rows] = new
    turned = square[...].T
    out_a[0] = turned[0:rank, 0:rows]
    out_b[0] = turned[rank:, 0:rows]

    gossip_copy.wait_send()

    @pl.when(crosses)
    def _():
        cross().wait_send()

    ab_mate(y_hi).wait_send()

    @pl.loop(0, half)
    def _(s):
        up(s).wait_send()
        ab_up(s).wait_send()

    @pl.loop(0, half - 1)
    def _(s):
        down(s).wait_send()
        ab_down(s).wait_send()

    @pl.loop(0, nz)
    def _(i):
        to_right(i).wait_send()
        to_left(i).wait_send()
        on_in(i).wait_send()
        across(i).wait_send()
        trade(i).wait_send()

    @pl.loop(1, nz)
    def _(i):
        give(i).wait_send()


def solution(mesh):
    n_gossip, n_zero = mesh.shape["gossip"], mesh.shape["zero"]
    nz = n_zero // 2
    half = nz // 2

    def per_device(queries, keys, values, pattern, out_weight, adapt_a, adapt_b):
        _, tokens, hd = queries.shape
        rows, rank = adapt_a.shape[1:]
        width = hd // 4
        dma = pltpu.SemaphoreType.DMA
        vmem = pltpu.VMEM
        whole = pl.BlockSpec(memory_space=pltpu.VMEM)
        place = pl.BlockSpec(memory_space=pl.ANY)
        flops = 2 * tokens * hd * (hd + 2 * tokens + 4 * rank)
        new_a, new_b = pl.pallas_call(
            functools.partial(kernel, nz, n_gossip, hd, rank),
            out_shape=(
                jax.ShapeDtypeStruct((1, rank, rows), F32),
                jax.ShapeDtypeStruct((1, rank, rows), F32),
            ),
            in_specs=[place, place, place, pl.BlockSpec(memory_space=pltpu.SMEM), place, whole, whole],
            out_specs=(whole, whole),
            scratch_shapes=[
                vmem((tokens, hd), BF16), vmem((tokens, hd), BF16), vmem((tokens, hd), BF16),
                vmem((4, nz, 2, rows, width), BF16),
                vmem((nz, 2, rows, 2 * rank), BF16), vmem((rows, 2 * rank), F32), vmem((2 * rank, 128), F32),
                vmem((TILE, 2 * TILE), F32), vmem((TILE, TILE), F32),
                vmem((hd, tokens), BF16), vmem((2 * rank, tokens), BF16), vmem((tokens, 2 * rank), BF16),
                vmem((2 * rank, tokens), F32), vmem((nz, 2 * rows, 2 * rank), F32),
                vmem((nz, 2, rows, 2 * rank), BF16), vmem((nz, rows, 2 * rank), BF16),
                vmem((nz, rows, 2 * rank), BF16), vmem((nz, rows, 2 * rank), BF16),
                vmem((rows, 2 * rank), F32), vmem((rows, 2 * rank), F32),
                dma((4,)), dma((2,)),
                dma((half + 1,)), dma((half + 1,)), dma((half + 1,)), dma((half + 1,)),
                dma((nz,)), dma((nz,)), dma((nz,)), dma((nz,)), dma((nz,)), dma((nz,)), dma((nz,)), dma((nz,)),
                dma((2,)), dma((half + 1,)), dma((half + 1,)), dma((half + 1,)), dma((half + 1,)),
                dma((nz,)), dma((nz,)), dma((nz,)), dma((nz,)), dma((2,)),
            ],
            compiler_params=pltpu.CompilerParams(
                collective_id=0, has_side_effects=True, vmem_limit_bytes=60 * 1024 * 1024
            ),
            cost_estimate=pl.CostEstimate(flops=flops, bytes_accessed=8 * tokens * hd, transcendentals=tokens * hd),
        )(queries, keys, values, pattern, out_weight.T, adapt_a.transpose(0, 2, 1), adapt_b)
        return new_a.transpose(0, 2, 1), new_b

    placed = (
        P(("gossip", "zero"), None, None),
        P(("gossip", "zero"), None, None),
        P(("gossip", "zero"), None, None),
        P(("gossip", "zero"), None, None),
        P(None, "zero"),
        P("gossip", "zero", None),
        P("gossip", None, "zero"),
    )
    return jax.shard_map(
        per_device,
        mesh=mesh,
        in_specs=placed,
        out_specs=(P("gossip", "zero", None), P("gossip", None, "zero")),
        check_vma=False,
    )
```

```python
import functools
import itertools
import math

import jax
import jax.numpy as jnp
from jax import lax
from jax.experimental import pallas as pl
from jax.experimental.pallas import tpu as pltpu
from jax.sharding import PartitionSpec as P

MESH = pl.DeviceIdType.MESH
HEAD = 128
TILE = 128
DIST = 2
RING = 4
PLAN = ((3, 0), (2, 0), (1, 3), (1, 1))
STEP_RATE = 0.5
SHARPNESS = 4.0
F32 = jnp.float32
BF16 = jnp.bfloat16


def nn(a, b):
    return lax.dot_general(a, b, (((1,), (0,)), ((), ())), preferred_element_type=F32)


def nt(a, b):
    return lax.dot_general(a, b, (((1,), (1,)), ((), ())), preferred_element_type=F32)


def tn(a, b):
    return lax.dot_general(a, b, (((0,), (0,)), ((), ())), preferred_element_type=F32)


def kernel(
    nz, n_gossip, hd, rank,
    q_hbm, k_hbm, v_hbm, pattern, w_hbm, a_ref, b_ref,
    out,
    q, k, v, wt, ab, abf, square, mask0, mask1, ctx, low, low_t, base, hid, grads, summed, theirs, landed, total, moved, partner,
    load_sem, opp_sem, zu_send, zu_recv, zd_send, zd_recv,
    right_send, left_send, left_recv, right_recv, on_send, on_recv, sib_send, sib_recv,
    abp_sem, abu_send, abu_recv, abd_send, abd_recv,
    yx_send, yx_recv, own_send, own_recv, gos_sem,
):
    half = nz // 2
    jump = half // 2 if half >= 4 else 0
    firsts = (1, jump) if jump else (1,)
    width = hd // 4
    rows = hd // (2 * nz)
    heads = hd // HEAD
    scale = 1.0 / math.sqrt(hd * rank)

    gossip, zero = lax.axis_index("gossip"), lax.axis_index("zero")
    core = lax.rem(gossip, 2)
    y_lo = lax.rem(lax.div(gossip, 2), 2)
    x = lax.div(gossip, 4)
    z = lax.div(zero, 2)
    y_hi = lax.rem(zero, 2)
    y = y_hi * 2 + y_lo
    place = core * y + (1 - core) * x

    def spread_device(step):
        xs = lax.rem(x + step + RING, RING)
        ys = lax.rem(y + step + RING, RING)
        g0, z0 = (xs * 2 + y_lo) * 2, zero
        g1, z1 = (x * 2 + lax.rem(ys, 2)) * 2 + 1, z * 2 + lax.div(ys, 2)
        return core * g1 + (1 - core) * g0, core * z1 + (1 - core) * z0

    def z_device(step):
        return gossip, lax.rem(z + step + nz, nz) * 2 + y_hi

    opposite = ((x * 2 + 1 - y_lo) * 2 + core, z * 2 + 1 - y_hi)
    sibling = ((x * 2 + y_lo) * 2 + 1 - core, zero)
    mate = (gossip, z * 2 + 1 - y_hi)
    right, left = spread_device(1), spread_device(-1)
    after = (lax.rem(gossip + DIST, n_gossip), zero)
    before = (lax.rem(gossip + n_gossip - DIST, n_gossip), zero)

    barrier = pltpu.get_barrier_semaphore()

    def greet(device):
        pl.semaphore_signal(barrier, inc=1, device_id=device, device_id_type=MESH)

    partners = [right, left, opposite, sibling, mate, after, before]
    for s in firsts:
        partners += [z_device(s), z_device(-s)] if 2 * s != nz else [z_device(s)]
    for device in partners:
        greet(device)

    def block(step):
        p = lax.rem(place + step + RING, RING)
        return core * 2 + lax.rem(p, 2), lax.div(p, 2)

    kb, r = block(0)
    crosses = (r == y_hi) & (core == 0)

    def plane(i):
        s, odd = lax.div(i + 1, 2), lax.rem(i, 2)
        return lax.rem(z + nz + s - 2 * odd * s, nz)

    def copy(src, dst, send, recv, device):
        return pltpu.make_async_remote_copy(
            src_ref=src, dst_ref=dst, send_sem=send, recv_sem=recv, device_id=device, device_id_type=MESH
        )

    loads = [
        pltpu.make_async_copy(q_hbm.at[0], q, load_sem.at[1]),
        pltpu.make_async_copy(k_hbm.at[0], k, load_sem.at[2]),
        pltpu.make_async_copy(v_hbm.at[0], v, load_sem.at[3]),
    ]
    own = pltpu.make_async_copy(
        w_hbm.at[:, pl.ds(pl.multiple_of(kb * width, 128), width)], wt.at[kb, z, r], load_sem.at[0]
    )

    @pl.when(r == y_hi)
    def _():
        own.start()

    for load in loads:
        load.start()

    square[...] = jnp.zeros_like(square)
    square[0:rank, 0:rows] = a_ref[0]
    square[rank:, 0:rows] = b_ref[0]
    abf[...] = square[...].T[0:rows]
    ab[z, y_hi] = abf[...].astype(BF16)

    key_at = lax.broadcasted_iota(jnp.int32, (TILE, 2 * TILE), 0)
    query_at = lax.broadcasted_iota(jnp.int32, (TILE, 2 * TILE), 1)
    sees = (pattern[0, 1, 1] == 0) | (pattern[0, 1, 2] == 0)
    far = jnp.where(sees, F32(0.0), F32(-1e30))
    mask0[...] = jnp.where(query_at < TILE, jnp.where(key_at <= query_at, F32(0.0), F32(-1e30)), far)
    mask1[...] = jnp.where(key_at <= query_at, F32(0.0), F32(-1e30))[:, 0:TILE]

    @pl.when(r == y_hi)
    def _():
        own.wait()

    pl.semaphore_wait(barrier, len(partners))

    def cross():
        return copy(wt.at[kb, z, r], wt.at[kb, z, r], opp_sem.at[0], opp_sem.at[1], opposite)

    middle = (rows // 2 + 15) // 16 * 16
    parts = ((0, middle), (middle, rows - middle))

    def up(s, slot, n):
        at = wt.at[kb, lax.rem(z - s + nz, nz), r, pl.ds(*parts[n])]
        return copy(at, at, zu_send.at[slot, n], zu_recv.at[slot, n], z_device(1))

    def down(s, slot, n):
        at = wt.at[kb, lax.rem(z + s, nz), r, pl.ds(*parts[n])]
        return copy(at, at, zd_send.at[slot, n], zd_recv.at[slot, n], z_device(-1))

    def to_right(i):
        at = wt.at[kb, plane(i), r]
        return copy(at, at, right_send.at[i], left_recv.at[i], right)

    def to_left(i):
        at = wt.at[kb, plane(i), r]
        return copy(at, at, left_send.at[i], right_recv.at[i], left)

    def from_left(i):
        n, m = block(-1)
        at = wt.at[n, plane(i), m]
        return copy(at, at, on_send.at[i], left_recv.at[i], right)

    def from_right(i):
        n, m = block(1)
        at = wt.at[n, plane(i), m]
        return copy(at, at, on_send.at[i], right_recv.at[i], left)

    def on_right(i):
        n, m = block(-1)
        at = wt.at[n, plane(i), m]
        return copy(at, at, on_send.at[i], on_recv.at[i], right)

    def on_left(i):
        n, m = block(1)
        at = wt.at[n, plane(i), m]
        return copy(at, at, on_send.at[i], on_recv.at[i], left)

    def on_in(i):
        n, m = block(2)
        at = wt.at[n, plane(i), m]
        return copy(at, at, on_send.at[i], on_recv.at[i], right)

    def across(i):
        at = wt.at[pl.ds(core * 2, 2), plane(i)]
        return copy(at, at, sib_send.at[i], sib_recv.at[i], sibling)

    def across_in(i):
        at = wt.at[pl.ds(2 - core * 2, 2), plane(i)]
        return copy(at, at, sib_send.at[i], sib_recv.at[i], sibling)

    def spread(i):
        to_right(i).start()
        to_left(i).start()

    def arrive(s):
        for n in range(2):
            up(s, s, n).wait_recv()
            if s < half:
                up(s, s + 1, n).start()
                down(s, s, n).wait_recv()
                if s < half - 1:
                    down(s, s + 1, n).start()
        spread(2 * s - 1)
        if s < half:
            spread(2 * s)

    def hand_on(s):
        i = max(2 * s - 1, 0)
        from_left(i).wait_recv()
        on_right(i).start()
        from_right(i).wait_recv()
        if 0 < s < half:
            from_right(2 * s).wait_recv()
            on_left(2 * s).start()
            from_left(2 * s).wait_recv()

    def share(s):
        on_in(max(2 * s - 1, 0)).wait_recv()
        across(max(2 * s - 1, 0)).start()
        if 0 < s < half:
            on_in(2 * s).wait_recv()
            across(2 * s).start()

    def ab_mate(which):
        at = ab.at[z, which]
        return copy(at, at, abp_sem.at[0], abp_sem.at[1], mate)

    def ab_up(s, step=1):
        at = ab.at[lax.rem(z - s + nz, nz)]
        return copy(at, at, abu_send.at[s + step], abu_recv.at[s + step], z_device(step))

    def ab_down(s, step=1):
        at = ab.at[lax.rem(z + s, nz)]
        return copy(at, at, abd_send.at[s + step], abd_recv.at[s + step], z_device(-step))

    def ab_in(s):
        at = ab.at[lax.rem(z - s + nz, nz)]
        copy(at, at, abu_send.at[s], abu_recv.at[s], z_device(1)).wait_recv()
        if s < half and s + 1 not in firsts:
            ab_up(s).start()
        if s < half:
            at = ab.at[lax.rem(z + s, nz)]
            copy(at, at, abd_send.at[s], abd_recv.at[s], z_device(-1)).wait_recv()
            if s < half - 1 and s + 1 not in firsts:
                ab_down(s).start()

    fold = F32(math.log2(math.e) / math.sqrt(HEAD))

    def attend(first, last):
        @pl.loop(first, last)
        def _(h):
            at = pl.ds(pl.multiple_of(h * HEAD, HEAD), HEAD)
            qh = q[:, at]
            s0 = nt(k[0:TILE, at], qh) * fold + mask0[...]
            s1 = nt(k[TILE:, at], qh[TILE:]) * fold + mask1[...]
            top0 = jnp.max(s0, axis=0, keepdims=True)
            top1 = jnp.max(s1, axis=0, keepdims=True)
            top1 = jnp.maximum(top0[:, TILE:], top1)
            e00 = jnp.exp2(s0[:, 0:TILE] - top0[:, 0:TILE])
            e01 = jnp.exp2(s0[:, TILE:] - top1)
            e11 = jnp.exp2(s1 - top1)
            total0 = jnp.sum(e00, axis=0, keepdims=True)
            total1 = jnp.sum(e01, axis=0, keepdims=True) + jnp.sum(e11, axis=0, keepdims=True)
            v0, v1 = v[0:TILE, at], v[TILE:, at]
            c0 = tn(v0, e00.astype(BF16)) / total0
            c1 = (tn(v0, e01.astype(BF16)) + tn(v1, e11.astype(BF16))) / total1
            ctx[at, 0:TILE] = c0.astype(BF16)
            ctx[at, TILE:] = c1.astype(BF16)

    def sides(part):
        nothing = jnp.zeros((2 * rank, 2 * TILE), F32)
        return jnp.concatenate([part, nothing, part], axis=0).T.astype(BF16)

    def adapt():
        both = tn(ab[...].reshape(hd, 2 * rank), ctx[...])
        low[0:rank] = jnp.zeros((rank, 2 * TILE), BF16)
        low[rank:] = both[0:rank].astype(BF16)
        low_t[...] = sides(low[rank:].astype(F32))

    def pack(g, w, wide):
        for m in range(2):
            lower = wide[m * rows + middle : (m + 1) * rows, 2 * rank :]
            if 2 * middle > rows:
                lower = jnp.concatenate([lower, jnp.zeros((2 * middle - rows, 2 * rank), F32)], axis=0)
            grads[g, w, m] = (scale * (wide[m * rows : m * rows + middle, 0 : 2 * rank] + lower)).astype(BF16)

    def trade(g, i):
        w = plane(i)
        return copy(grads.at[g, w, 1 - y_hi], theirs.at[g, w], yx_send.at[g, i], yx_recv.at[g, i], mate)

    def give(g, i):
        w = plane(i)
        owner = (gossip, w * 2 + y_hi)
        return copy(summed.at[g, w], landed.at[g, z], own_send.at[g, i], own_recv.at[g, z], owner)

    def take(g, i):
        w = plane(i)
        owner = (gossip, w * 2 + y_hi)
        return copy(summed.at[g, w], landed.at[g, w], own_send.at[g, i], own_recv.at[g, w], owner)

    def pass_on(g, i):
        w = plane(i)
        trade(g, i).wait_recv()
        summed[g, w] = (grads[g, w, y_hi].astype(F32) + theirs[g, w].astype(F32)).astype(BF16)
        give(g, i).start()

    def collect(g):
        trade(g, 0).wait_recv()
        total[g] = grads[g, z, y_hi].astype(F32) + theirs[g, z].astype(F32)

        @pl.loop(1, nz)
        def _(i):
            take(g, i).wait_recv()
            total[g] += landed[g, plane(i)].astype(F32)

    based = []

    def product(planes):
        weights = [jnp.concatenate([wt[n, w].reshape(2 * rows, width) for w in planes], axis=0) for n in range(4)]
        return nn(jnp.concatenate(weights, axis=1), ctx[...])

    def prepare(s):
        members = [max(2 * s - 1, 0)] + ([2 * s] if 0 < s < half else [])
        for i in members:
            across_in(i).wait_recv()
        planes = [plane(i) for i in members]
        out = product(planes)
        for n, w in enumerate(planes):
            base[w] = out[n * 2 * rows : (n + 1) * 2 * rows]
        based.append(s)

    def project(s):
        members = [max(2 * s - 1, 0)] + ([2 * s] if 0 < s < half else [])
        if s not in based:
            for i in members:
                across_in(i).wait_recv()
        planes = [plane(i) for i in members]

        def rows_of(blocks):
            return jnp.concatenate([b.reshape(2 * rows, b.shape[-1]) for b in blocks], axis=0)

        factors = rows_of([ab[w] for w in planes])
        out = scale * nn(factors, low[...])
        if s in based:
            out += rows_of([base[w] for w in planes])
        else:
            out += product(planes)
        slope = jnp.tanh(SHARPNESS * out).astype(BF16)
        hid[...] += tn(factors, slope)
        wide = nn(slope, low_t[...])
        for n, w in enumerate(planes):
            pack(0, w, wide[n * 2 * rows : (n + 1) * 2 * rows])
            trade(0, members[n]).start()

    @pl.when(crosses)
    def _():
        cross().start()

    ab_mate(y_hi).start()

    @pl.when(r != y_hi)
    def _():
        cross().wait_recv()

    for n in range(2):
        up(0, 1, n).start()
        if half > 1:
            down(0, 1, n).start()
    spread(0)
    for load in loads:
        load.wait()
    hid[...] = jnp.zeros_like(hid)
    cut = [heads * n // 5 for n in range(6)]
    attend(cut[0], cut[1])
    ab_mate(1 - y_hi).wait_recv()
    for s in reversed(firsts):
        ab_up(0, s).start()
        if s < half:
            ab_down(0, s).start()
    attend(cut[1], cut[2])
    chains = [range(a, b) for a, b in zip(firsts, (*firsts[1:], half + 1))]
    ticks = [[s for s in tick if s is not None] for tick in itertools.zip_longest(*chains)]
    todo, traded = [], []

    def work_off(count):
        for s in todo[:count]:
            project(s)
            traded.append([i for i in ((2 * s - 1, 2 * s) if s < half else (2 * s - 1,)) if i > 0])
        del todo[:count]

    def pass_off(count):
        for group in traded[:count]:
            for i in group:
                pass_on(0, i)
        del traded[:count]

    for t in range(1, half + 1):
        arrive(t)
        if t <= len(ticks):
            for s in ticks[t - 1]:
                ab_in(s)
        if t <= 3:
            attend(cut[t + 1], cut[t + 2])
        if t == len(ticks):
            adapt()
        hand_on(t - 1)
        if t >= 2:
            share(t - 2)
            todo.append(t - 2)
        if 3 <= t < half:
            prepare(t - 3)
        if t > len(ticks):
            work_off(PLAN[t - len(ticks) - 1][0])
            pass_off(PLAN[t - len(ticks) - 1][1])
    for t in range(half, 3):
        attend(cut[t + 2], cut[t + 3])
    hand_on(half)
    share(half - 1)
    todo.append(half - 1)
    pass_off(1)
    work_off(len(todo) - 1)
    pass_off(1)
    share(half)
    todo.append(half)
    work_off(1)
    pass_off(2)
    work_off(len(todo))

    hid_t = sides(hid[rank:])

    @pl.loop(0, nz)
    def _(n):
        i = nz - 1 - n
        w = plane(i)
        part = ctx[pl.ds(pl.multiple_of(w * 2 * rows, 2 * rows), 2 * rows)]
        pack(1, w, nn(part, hid_t))
        trade(1, i).start()

    pass_off(len(traded))

    @pl.loop(0, nz - 1)
    def _(n):
        pass_on(1, nz - 1 - n)

    collect(0)
    collect(1)

    def unpack(g, turn):
        straight, turned = total[g], pltpu.roll(total[g], rank, 1)
        if turn:
            straight, turned = turned, straight
        return jnp.concatenate([straight, turned[0 : rows - middle]], axis=0)

    column = lax.broadcasted_iota(jnp.int32, (rows, 2 * rank), 1)
    gradient = jnp.where(column < rank, unpack(1, False), unpack(0, True))
    moved[...] = abf[...] - STEP_RATE * gradient
    gossip_copy = copy(moved, partner, gos_sem.at[0], gos_sem.at[1], after)
    gossip_copy.start()
    gossip_copy.wait_recv()
    new = 0.5 * (moved[...] + partner[...])
    square[...] = jnp.zeros_like(square)
    square[0:rows] = new
    turned = square[...].T
    out[...] = turned[:, 0:rows]

    gossip_copy.wait_send()

    @pl.when(crosses)
    def _():
        cross().wait_send()

    ab_mate(y_hi).wait_send()

    @pl.loop(0, half)
    def _(s):
        for n in range(2):
            up(s, s + 1, n).wait_send()
        ab_up(s).wait_send()

    @pl.loop(0, half - 1)
    def _(s):
        for n in range(2):
            down(s, s + 1, n).wait_send()
        ab_down(s).wait_send()

    @pl.loop(0, nz)
    def _(i):
        to_right(i).wait_send()
        to_left(i).wait_send()
        on_in(i).wait_send()
        across(i).wait_send()
        trade(0, i).wait_send()
        trade(1, i).wait_send()

    @pl.loop(1, nz)
    def _(i):
        give(0, i).wait_send()
        give(1, i).wait_send()


def part_in_two(rank, both, upper, lower):
    upper[0] = both[0:rank]
    lower[0] = both[rank:]


def solution(mesh):
    n_gossip, n_zero = mesh.shape["gossip"], mesh.shape["zero"]
    nz = n_zero // 2
    half = nz // 2

    def per_device(queries, keys, values, pattern, out_weight, adapt_a, adapt_b):
        _, tokens, hd = queries.shape
        rows, rank = adapt_a.shape[1:]
        width = hd // 4
        middle = (rows // 2 + 15) // 16 * 16
        dma = pltpu.SemaphoreType.DMA
        vmem = pltpu.VMEM
        whole = pl.BlockSpec(memory_space=pltpu.VMEM)
        place = pl.BlockSpec(memory_space=pl.ANY)
        flops = 2 * tokens * hd * (hd + 2 * tokens + 4 * rank)
        new = pl.pallas_call(
            functools.partial(kernel, nz, n_gossip, hd, rank),
            out_shape=jax.ShapeDtypeStruct((2 * rank, rows), F32),
            in_specs=[place, place, place, pl.BlockSpec(memory_space=pltpu.SMEM), place, whole, whole],
            out_specs=whole,
            scratch_shapes=[
                vmem((tokens, hd), BF16), vmem((tokens, hd), BF16), vmem((tokens, hd), BF16),
                vmem((4, nz, 2, rows, width), BF16),
                vmem((nz, 2, rows, 2 * rank), BF16), vmem((rows, 2 * rank), F32), vmem((2 * rank, 128), F32),
                vmem((TILE, 2 * TILE), F32), vmem((TILE, TILE), F32),
                vmem((hd, tokens), BF16), vmem((2 * rank, tokens), BF16), vmem((tokens, 4 * rank), BF16),
                vmem((nz, 2 * rows, tokens), F32), vmem((2 * rank, tokens), F32), vmem((2, nz, 2, middle, 2 * rank), BF16),
                vmem((2, nz, middle, 2 * rank), BF16), vmem((2, nz, middle, 2 * rank), BF16),
                vmem((2, nz, middle, 2 * rank), BF16), vmem((2, middle, 2 * rank), F32),
                vmem((rows, 2 * rank), F32), vmem((rows, 2 * rank), F32),
                dma((4,)), dma((2,)),
                dma((half + 1, 2)), dma((half + 1, 2)), dma((half + 1, 2)), dma((half + 1, 2)),
                dma((nz,)), dma((nz,)), dma((nz,)), dma((nz,)), dma((nz,)), dma((nz,)), dma((nz,)), dma((nz,)),
                dma((2,)), dma((half + 1,)), dma((half + 1,)), dma((half + 1,)), dma((half + 1,)),
                dma((2, nz)), dma((2, nz)), dma((2, nz)), dma((2, nz)), dma((2,)),
            ],
            compiler_params=pltpu.CompilerParams(
                collective_id=0, has_side_effects=True, vmem_limit_bytes=60 * 1024 * 1024
            ),
            cost_estimate=pl.CostEstimate(flops=flops, bytes_accessed=8 * tokens * hd, transcendentals=tokens * hd),
        )(queries, keys, values, pattern, out_weight.T, adapt_a.transpose(0, 2, 1), adapt_b)
        half_shape = jax.ShapeDtypeStruct((1, rank, rows), F32)
        new_a, new_b = pl.pallas_call(
            functools.partial(part_in_two, rank), out_shape=(half_shape, half_shape), in_specs=[whole], out_specs=(whole, whole)
        )(new)
        return new_a.transpose(0, 2, 1), new_b

    placed = (
        P(("gossip", "zero"), None, None),
        P(("gossip", "zero"), None, None),
        P(("gossip", "zero"), None, None),
        P(("gossip", "zero"), None, None),
        P(None, "zero"),
        P("gossip", "zero", None),
        P("gossip", None, "zero"),
    )
    return jax.shard_map(
        per_device,
        mesh=mesh,
        in_specs=placed,
        out_specs=(P("gossip", "zero", None), P("gossip", None, "zero")),
        check_vma=False,
    )
```

```python
import functools
import itertools
import math

import jax
import jax.numpy as jnp
from jax import lax
from jax.experimental import pallas as pl
from jax.experimental.pallas import tpu as pltpu
from jax.sharding import PartitionSpec as P

MESH = pl.DeviceIdType.MESH
HEAD = 128
TILE = 128
DIST = 2
RING = 4
PLAN = ((3, 0), (2, 0), (1, 3), (1, 1))
STEP_RATE = 0.5
SHARPNESS = 4.0
F32 = jnp.float32
BF16 = jnp.bfloat16


def nn(a, b):
    return lax.dot_general(a, b, (((1,), (0,)), ((), ())), preferred_element_type=F32)


def nt(a, b):
    return lax.dot_general(a, b, (((1,), (1,)), ((), ())), preferred_element_type=F32)


def tn(a, b):
    return lax.dot_general(a, b, (((0,), (0,)), ((), ())), preferred_element_type=F32)


def kernel(
    nz, n_gossip, hd, rank,
    q_hbm, k_hbm, v_hbm, pattern_hbm, w_hbm, a_hbm, b_hbm,
    out,
    q, k, v, pattern, factors_in, wt, ab, abf, square, mask0, mask1, ctx, low, low_t, base, hid, grads, summed, theirs, landed, total, moved, partner,
    load_sem, opp_sem, zu_send, zu_recv, zd_send, zd_recv,
    right_send, left_send, left_recv, right_recv, on_send, on_recv, sib_send, sib_recv,
    abp_sem, abu_send, abu_recv, abd_send, abd_recv,
    yx_send, yx_recv, own_send, own_recv, gos_sem,
):
    half = nz // 2
    jump = half // 2 if half >= 4 else 0
    firsts = (1, jump) if jump else (1,)
    width = hd // 4
    rows = hd // (2 * nz)
    heads = hd // HEAD
    scale = 1.0 / math.sqrt(hd * rank)

    gossip, zero = lax.axis_index("gossip"), lax.axis_index("zero")
    core = lax.rem(gossip, 2)
    y_lo = lax.rem(lax.div(gossip, 2), 2)
    x = lax.div(gossip, 4)
    z = lax.div(zero, 2)
    y_hi = lax.rem(zero, 2)
    y = y_hi * 2 + y_lo
    place = core * y + (1 - core) * x

    def spread_device(step):
        xs = lax.rem(x + step + RING, RING)
        ys = lax.rem(y + step + RING, RING)
        g0, z0 = (xs * 2 + y_lo) * 2, zero
        g1, z1 = (x * 2 + lax.rem(ys, 2)) * 2 + 1, z * 2 + lax.div(ys, 2)
        return core * g1 + (1 - core) * g0, core * z1 + (1 - core) * z0

    def z_device(step):
        return gossip, lax.rem(z + step + nz, nz) * 2 + y_hi

    opposite = ((x * 2 + 1 - y_lo) * 2 + core, z * 2 + 1 - y_hi)
    sibling = ((x * 2 + y_lo) * 2 + 1 - core, zero)
    mate = (gossip, z * 2 + 1 - y_hi)
    right, left = spread_device(1), spread_device(-1)
    after = (lax.rem(gossip + DIST, n_gossip), zero)
    before = (lax.rem(gossip + n_gossip - DIST, n_gossip), zero)

    barrier = pltpu.get_barrier_semaphore()

    def greet(device):
        pl.semaphore_signal(barrier, inc=1, device_id=device, device_id_type=MESH)

    partners = [right, left, opposite, sibling, mate, after, before]
    for s in firsts:
        partners += [z_device(s), z_device(-s)] if 2 * s != nz else [z_device(s)]
    for device in partners:
        greet(device)

    def block(step):
        p = lax.rem(place + step + RING, RING)
        return core * 2 + lax.rem(p, 2), lax.div(p, 2)

    kb, r = block(0)
    crosses = (r == y_hi) & (core == 0)

    def plane(i):
        s, odd = lax.div(i + 1, 2), lax.rem(i, 2)
        return lax.rem(z + nz + s - 2 * odd * s, nz)

    def copy(src, dst, send, recv, device):
        return pltpu.make_async_remote_copy(
            src_ref=src, dst_ref=dst, send_sem=send, recv_sem=recv, device_id=device, device_id_type=MESH
        )

    loads = [
        pltpu.make_async_copy(q_hbm.at[0], q, load_sem.at[1]),
        pltpu.make_async_copy(k_hbm.at[0], k, load_sem.at[2]),
        pltpu.make_async_copy(v_hbm.at[0], v, load_sem.at[3]),
    ]
    own = pltpu.make_async_copy(
        w_hbm.at[:, pl.ds(pl.multiple_of(kb * width, 128), width)], wt.at[kb, z, r], load_sem.at[0]
    )

    @pl.when(r == y_hi)
    def _():
        own.start()

    small = [
        pltpu.make_async_copy(a_hbm.at[0], factors_in.at[0], load_sem.at[4]),
        pltpu.make_async_copy(b_hbm.at[0], factors_in.at[1], load_sem.at[5]),
        pltpu.make_async_copy(pattern_hbm, pattern, load_sem.at[6]),
    ]
    for load in [*small, *loads]:
        load.start()

    square[...] = jnp.zeros_like(square)
    for load in small:
        load.wait()
    square[0:rank, 0:rows] = factors_in[0]
    square[rank:, 0:rows] = factors_in[1]
    abf[...] = square[...].T[0:rows]
    ab[z, y_hi] = abf[...].astype(BF16)

    key_at = lax.broadcasted_iota(jnp.int32, (TILE, 2 * TILE), 0)
    query_at = lax.broadcasted_iota(jnp.int32, (TILE, 2 * TILE), 1)
    sees = (pattern[0, 1, 1] == 0) | (pattern[0, 1, 2] == 0)
    far = jnp.where(sees, F32(0.0), F32(-1e30))
    mask0[...] = jnp.where(query_at < TILE, jnp.where(key_at <= query_at, F32(0.0), F32(-1e30)), far)
    mask1[...] = jnp.where(key_at <= query_at, F32(0.0), F32(-1e30))[:, 0:TILE]

    @pl.when(r == y_hi)
    def _():
        own.wait()

    pl.semaphore_wait(barrier, len(partners))

    def cross():
        return copy(wt.at[kb, z, r], wt.at[kb, z, r], opp_sem.at[0], opp_sem.at[1], opposite)

    middle = (rows // 2 + 15) // 16 * 16
    parts = ((0, middle), (middle, rows - middle))

    def up(s, slot, n):
        at = wt.at[kb, lax.rem(z - s + nz, nz), r, pl.ds(*parts[n])]
        return copy(at, at, zu_send.at[slot, n], zu_recv.at[slot, n], z_device(1))

    def down(s, slot, n):
        at = wt.at[kb, lax.rem(z + s, nz), r, pl.ds(*parts[n])]
        return copy(at, at, zd_send.at[slot, n], zd_recv.at[slot, n], z_device(-1))

    def to_right(i):
        at = wt.at[kb, plane(i), r]
        return copy(at, at, right_send.at[i], left_recv.at[i], right)

    def to_left(i):
        at = wt.at[kb, plane(i), r]
        return copy(at, at, left_send.at[i], right_recv.at[i], left)

    def from_left(i):
        n, m = block(-1)
        at = wt.at[n, plane(i), m]
        return copy(at, at, on_send.at[i], left_recv.at[i], right)

    def from_right(i):
        n, m = block(1)
        at = wt.at[n, plane(i), m]
        return copy(at, at, on_send.at[i], right_recv.at[i], left)

    def on_right(i):
        n, m = block(-1)
        at = wt.at[n, plane(i), m]
        return copy(at, at, on_send.at[i], on_recv.at[i], right)

    def on_left(i):
        n, m = block(1)
        at = wt.at[n, plane(i), m]
        return copy(at, at, on_send.at[i], on_recv.at[i], left)

    def on_in(i):
        n, m = block(2)
        at = wt.at[n, plane(i), m]
        return copy(at, at, on_send.at[i], on_recv.at[i], right)

    def across(i):
        at = wt.at[pl.ds(core * 2, 2), plane(i)]
        return copy(at, at, sib_send.at[i], sib_recv.at[i], sibling)

    def across_in(i):
        at = wt.at[pl.ds(2 - core * 2, 2), plane(i)]
        return copy(at, at, sib_send.at[i], sib_recv.at[i], sibling)

    def spread(i):
        to_right(i).start()
        to_left(i).start()

    def arrive(s):
        for n in range(2):
            if s < half or n == 0:
                up(s, s, n).wait_recv()
            if s < half - 1 or (s < half and n == 0):
                up(s, s + 1, n).start()
            if s < half or n == 1:
                down(s, s, n).wait_recv()
            if s < half - 1 or (s < half and n == 1):
                down(s, s + 1, n).start()
        spread(2 * s - 1)
        if s < half:
            spread(2 * s)

    def hand_on(s):
        i = max(2 * s - 1, 0)
        from_left(i).wait_recv()
        on_right(i).start()
        from_right(i).wait_recv()
        if 0 < s < half:
            from_right(2 * s).wait_recv()
            on_left(2 * s).start()
            from_left(2 * s).wait_recv()

    def share(s):
        on_in(max(2 * s - 1, 0)).wait_recv()
        across(max(2 * s - 1, 0)).start()
        if 0 < s < half:
            on_in(2 * s).wait_recv()
            across(2 * s).start()

    def ab_mate(which):
        at = ab.at[z, which]
        return copy(at, at, abp_sem.at[0], abp_sem.at[1], mate)

    def ab_up(s, step=1):
        at = ab.at[lax.rem(z - s + nz, nz)]
        return copy(at, at, abu_send.at[s + step], abu_recv.at[s + step], z_device(step))

    def ab_down(s, step=1):
        at = ab.at[lax.rem(z + s, nz)]
        return copy(at, at, abd_send.at[s + step], abd_recv.at[s + step], z_device(-step))

    def ab_in(s):
        at = ab.at[lax.rem(z - s + nz, nz)]
        copy(at, at, abu_send.at[s], abu_recv.at[s], z_device(1)).wait_recv()
        if s < half and s + 1 not in firsts:
            ab_up(s).start()
        if s < half:
            at = ab.at[lax.rem(z + s, nz)]
            copy(at, at, abd_send.at[s], abd_recv.at[s], z_device(-1)).wait_recv()
            if s < half - 1 and s + 1 not in firsts:
                ab_down(s).start()

    fold = F32(math.log2(math.e) / math.sqrt(HEAD))

    def attend(first, last):
        @pl.loop(first, last)
        def _(h):
            at = pl.ds(pl.multiple_of(h * HEAD, HEAD), HEAD)
            qh = q[:, at]
            s0 = nt(k[0:TILE, at], qh) * fold + mask0[...]
            s1 = nt(k[TILE:, at], qh[TILE:]) * fold + mask1[...]
            top0 = jnp.max(s0, axis=0, keepdims=True)
            top1 = jnp.max(s1, axis=0, keepdims=True)
            top1 = jnp.maximum(top0[:, TILE:], top1)
            e00 = jnp.exp2(s0[:, 0:TILE] - top0[:, 0:TILE])
            e01 = jnp.exp2(s0[:, TILE:] - top1)
            e11 = jnp.exp2(s1 - top1)
            total0 = jnp.sum(e00, axis=0, keepdims=True)
            total1 = jnp.sum(e01, axis=0, keepdims=True) + jnp.sum(e11, axis=0, keepdims=True)
            part0, part1 = 1.0 / total0, 1.0 / total1
            v0, v1 = v[0:TILE, at], v[TILE:, at]
            c0 = tn(v0, (e00 * part0).astype(BF16))
            c1 = tn(v0, (e01 * part1).astype(BF16)) + tn(v1, (e11 * part1).astype(BF16))
            ctx[at, 0:TILE] = c0.astype(BF16)
            ctx[at, TILE:] = c1.astype(BF16)

    def sides(part):
        nothing = jnp.zeros((2 * rank, 2 * TILE), F32)
        return jnp.concatenate([part, nothing, part], axis=0).T.astype(BF16)

    def adapt():
        both = tn(ab[...].reshape(hd, 2 * rank), ctx[...])
        low[0:rank] = jnp.zeros((rank, 2 * TILE), BF16)
        low[rank:] = both[0:rank].astype(BF16)
        low_t[...] = sides(low[rank:].astype(F32))

    def pack(g, w, wide):
        for m in range(2):
            lower = wide[m * rows + middle : (m + 1) * rows, 2 * rank :]
            if 2 * middle > rows:
                lower = jnp.concatenate([lower, jnp.zeros((2 * middle - rows, 2 * rank), F32)], axis=0)
            grads[g, w, m] = (scale * (wide[m * rows : m * rows + middle, 0 : 2 * rank] + lower)).astype(BF16)

    def trade(g, i):
        w = plane(i)
        return copy(grads.at[g, w, 1 - y_hi], theirs.at[g, w], yx_send.at[g, i], yx_recv.at[g, i], mate)

    def give(g, i):
        w = plane(i)
        owner = (gossip, w * 2 + y_hi)
        return copy(summed.at[g, w], landed.at[g, z], own_send.at[g, i], own_recv.at[g, z], owner)

    def take(g, i):
        w = plane(i)
        owner = (gossip, w * 2 + y_hi)
        return copy(summed.at[g, w], landed.at[g, w], own_send.at[g, i], own_recv.at[g, w], owner)

    def pass_on(g, i):
        w = plane(i)
        trade(g, i).wait_recv()
        summed[g, w] = (grads[g, w, y_hi].astype(F32) + theirs[g, w].astype(F32)).astype(BF16)
        give(g, i).start()

    def collect(g):
        trade(g, 0).wait_recv()
        total[g] = grads[g, z, y_hi].astype(F32) + theirs[g, z].astype(F32)

        @pl.loop(1, nz)
        def _(i):
            take(g, i).wait_recv()
            total[g] += landed[g, plane(i)].astype(F32)

    based = []

    def product(planes):
        weights = [jnp.concatenate([wt[n, w].reshape(2 * rows, width) for w in planes], axis=0) for n in range(4)]
        return nn(jnp.concatenate(weights, axis=1), ctx[...])

    def prepare(s):
        members = [max(2 * s - 1, 0)] + ([2 * s] if 0 < s < half else [])
        for i in members:
            across_in(i).wait_recv()
        planes = [plane(i) for i in members]
        out = product(planes)
        for n, w in enumerate(planes):
            base[w] = out[n * 2 * rows : (n + 1) * 2 * rows]
        based.append(s)

    def project(s):
        members = [max(2 * s - 1, 0)] + ([2 * s] if 0 < s < half else [])
        if s not in based:
            for i in members:
                across_in(i).wait_recv()
        planes = [plane(i) for i in members]

        def rows_of(blocks):
            return jnp.concatenate([b.reshape(2 * rows, b.shape[-1]) for b in blocks], axis=0)

        factors = rows_of([ab[w] for w in planes])
        out = scale * nn(factors, low[...])
        if s in based:
            out += rows_of([base[w] for w in planes])
        else:
            out += product(planes)
        slope = jnp.tanh(SHARPNESS * out).astype(BF16)
        hid[...] += tn(factors, slope)
        wide = nn(slope, low_t[...])
        for n, w in enumerate(planes):
            pack(0, w, wide[n * 2 * rows : (n + 1) * 2 * rows])
            trade(0, members[n]).start()

    @pl.when(crosses)
    def _():
        cross().start()

    ab_mate(y_hi).start()

    @pl.when(r != y_hi)
    def _():
        cross().wait_recv()

    for n in range(2):
        up(0, 1, n).start()
        down(0, 1, n).start()
    spread(0)
    for load in loads:
        load.wait()
    hid[...] = jnp.zeros_like(hid)
    cut = [heads * n // 5 for n in range(6)]
    attend(cut[0], cut[1])
    ab_mate(1 - y_hi).wait_recv()
    for s in reversed(firsts):
        ab_up(0, s).start()
        if s < half:
            ab_down(0, s).start()
    attend(cut[1], cut[2])
    chains = [range(a, b) for a, b in zip(firsts, (*firsts[1:], half + 1))]
    ticks = [[s for s in tick if s is not None] for tick in itertools.zip_longest(*chains)]
    todo, traded = [], []

    def work_off(count):
        for s in todo[:count]:
            project(s)
            traded.append([i for i in ((2 * s - 1, 2 * s) if s < half else (2 * s - 1,)) if i > 0])
        del todo[:count]

    def pass_off(count):
        for group in traded[:count]:
            for i in group:
                pass_on(0, i)
        del traded[:count]

    for t in range(1, half + 1):
        arrive(t)
        if t <= len(ticks):
            for s in ticks[t - 1]:
                ab_in(s)
        if t <= 3:
            attend(cut[t + 1], cut[t + 2])
        if t == len(ticks):
            adapt()
        hand_on(t - 1)
        if t >= 2:
            share(t - 2)
            todo.append(t - 2)
        if 3 <= t < half:
            prepare(t - 3)
        if t > len(ticks):
            work_off(PLAN[t - len(ticks) - 1][0])
            pass_off(PLAN[t - len(ticks) - 1][1])
    for t in range(half, 3):
        attend(cut[t + 2], cut[t + 3])
    hand_on(half)
    share(half - 1)
    todo.append(half - 1)
    pass_off(1)
    work_off(len(todo) - 1)
    pass_off(1)
    share(half)
    todo.append(half)
    work_off(1)
    pass_off(2)
    work_off(len(todo))

    hid_t = sides(hid[rank:])

    def send_a(n):
        i = nz - 1 - n
        w = plane(i)
        part = ctx[pl.ds(pl.multiple_of(w * 2 * rows, 2 * rows), 2 * rows)]
        pack(1, w, nn(part, hid_t))
        trade(1, i).start()

    pl.loop(0, half)(send_a)
    pass_off(len(traded))
    pl.loop(half, nz)(send_a)

    @pl.loop(0, nz - 1)
    def _(n):
        pass_on(1, nz - 1 - n)

    collect(0)
    collect(1)

    def unpack(g, turn):
        straight, turned = total[g], pltpu.roll(total[g], rank, 1)
        if turn:
            straight, turned = turned, straight
        return jnp.concatenate([straight, turned[0 : rows - middle]], axis=0)

    column = lax.broadcasted_iota(jnp.int32, (rows, 2 * rank), 1)
    gradient = jnp.where(column < rank, unpack(1, False), unpack(0, True))
    moved[...] = abf[...] - STEP_RATE * gradient
    gossip_copy = copy(moved, partner, gos_sem.at[0], gos_sem.at[1], after)
    gossip_copy.start()
    gossip_copy.wait_recv()
    new = 0.5 * (moved[...] + partner[...])
    square[...] = jnp.zeros_like(square)
    square[0:rows] = new
    turned = square[...].T
    out[...] = turned[:, 0:rows]

    gossip_copy.wait_send()

    @pl.when(crosses)
    def _():
        cross().wait_send()

    ab_mate(y_hi).wait_send()

    up(half - 1, half, 0).wait_send()
    down(half - 1, half, 1).wait_send()

    @pl.loop(0, half)
    def _(s):
        ab_up(s).wait_send()

    @pl.loop(0, half - 1)
    def _(s):
        for n in range(2):
            up(s, s + 1, n).wait_send()
            down(s, s + 1, n).wait_send()
        ab_down(s).wait_send()

    @pl.loop(0, nz)
    def _(i):
        to_right(i).wait_send()
        to_left(i).wait_send()
        on_in(i).wait_send()
        across(i).wait_send()
        trade(0, i).wait_send()
        trade(1, i).wait_send()

    @pl.loop(1, nz)
    def _(i):
        give(0, i).wait_send()
        give(1, i).wait_send()


def part_in_two(rank, both, upper, lower):
    upper[0] = both[0:rank]
    lower[0] = both[rank:]


def solution(mesh):
    n_gossip, n_zero = mesh.shape["gossip"], mesh.shape["zero"]
    nz = n_zero // 2
    half = nz // 2

    def per_device(queries, keys, values, pattern, out_weight, adapt_a, adapt_b):
        _, tokens, hd = queries.shape
        rows, rank = adapt_a.shape[1:]
        width = hd // 4
        middle = (rows // 2 + 15) // 16 * 16
        dma = pltpu.SemaphoreType.DMA
        vmem = pltpu.VMEM
        whole = pl.BlockSpec(memory_space=pltpu.VMEM)
        place = pl.BlockSpec(memory_space=pl.ANY)
        flops = 2 * tokens * hd * (hd + 2 * tokens + 4 * rank)
        new = pl.pallas_call(
            functools.partial(kernel, nz, n_gossip, hd, rank),
            out_shape=jax.ShapeDtypeStruct((2 * rank, rows), F32),
            in_specs=[place] * 7,
            out_specs=whole,
            scratch_shapes=[
                vmem((tokens, hd), BF16), vmem((tokens, hd), BF16), vmem((tokens, hd), BF16),
                pltpu.SMEM(pattern.shape, jnp.int32), vmem((2, rank, rows), F32),
                vmem((4, nz, 2, rows, width), BF16),
                vmem((nz, 2, rows, 2 * rank), BF16), vmem((rows, 2 * rank), F32), vmem((2 * rank, 128), F32),
                vmem((TILE, 2 * TILE), F32), vmem((TILE, TILE), F32),
                vmem((hd, tokens), BF16), vmem((2 * rank, tokens), BF16), vmem((tokens, 4 * rank), BF16),
                vmem((nz, 2 * rows, tokens), F32), vmem((2 * rank, tokens), F32), vmem((2, nz, 2, middle, 2 * rank), BF16),
                vmem((2, nz, middle, 2 * rank), BF16), vmem((2, nz, middle, 2 * rank), BF16),
                vmem((2, nz, middle, 2 * rank), BF16), vmem((2, middle, 2 * rank), F32),
                vmem((rows, 2 * rank), F32), vmem((rows, 2 * rank), F32),
                dma((7,)), dma((2,)),
                dma((half + 1, 2)), dma((half + 1, 2)), dma((half + 1, 2)), dma((half + 1, 2)),
                dma((nz,)), dma((nz,)), dma((nz,)), dma((nz,)), dma((nz,)), dma((nz,)), dma((nz,)), dma((nz,)),
                dma((2,)), dma((half + 1,)), dma((half + 1,)), dma((half + 1,)), dma((half + 1,)),
                dma((2, nz)), dma((2, nz)), dma((2, nz)), dma((2, nz)), dma((2,)),
            ],
            compiler_params=pltpu.CompilerParams(
                collective_id=0, has_side_effects=True, vmem_limit_bytes=60 * 1024 * 1024
            ),
            cost_estimate=pl.CostEstimate(flops=flops, bytes_accessed=8 * tokens * hd, transcendentals=tokens * hd),
        )(queries, keys, values, pattern, out_weight.T, adapt_a.transpose(0, 2, 1), adapt_b)
        half_shape = jax.ShapeDtypeStruct((1, rank, rows), F32)
        new_a, new_b = pl.pallas_call(
            functools.partial(part_in_two, rank), out_shape=(half_shape, half_shape), in_specs=[whole], out_specs=(whole, whole)
        )(new)
        return new_a.transpose(0, 2, 1), new_b

    placed = (
        P(("gossip", "zero"), None, None),
        P(("gossip", "zero"), None, None),
        P(("gossip", "zero"), None, None),
        P(("gossip", "zero"), None, None),
        P(None, "zero"),
        P("gossip", "zero", None),
        P("gossip", None, "zero"),
    )
    return jax.shard_map(
        per_device,
        mesh=mesh,
        in_specs=placed,
        out_specs=(P("gossip", "zero", None), P("gossip", None, "zero")),
        check_vma=False,
    )
```

```python
import functools
import itertools
import math

import jax
import jax.numpy as jnp
from jax import lax
from jax.experimental import pallas as pl
from jax.experimental.pallas import tpu as pltpu
from jax.sharding import PartitionSpec as P

MESH = pl.DeviceIdType.MESH
HEAD = 128
TILE = 128
DIST = 2
RING = 4
PLAN = ((3, 0), (2, 0), (1, 3), (1, 1))
STEP_RATE = 0.5
SHARPNESS = 4.0
F32 = jnp.float32
BF16 = jnp.bfloat16


def nn(a, b):
    return lax.dot_general(a, b, (((1,), (0,)), ((), ())), preferred_element_type=F32)


def nt(a, b):
    return lax.dot_general(a, b, (((1,), (1,)), ((), ())), preferred_element_type=F32)


def tn(a, b):
    return lax.dot_general(a, b, (((0,), (0,)), ((), ())), preferred_element_type=F32)


def kernel(
    nz, n_gossip, hd, rank,
    q_hbm, k_hbm, v_hbm, pattern_hbm, w_hbm, a_hbm, b_hbm,
    out,
    q, k, v, pattern, factors_in, wt, ab, abf, square, mask0, mask1, ctx, low, low_t, base, hid, grads, summed, theirs, landed, total, moved, partner,
    load_sem, opp_sem, zu_send, zu_recv, zd_send, zd_recv,
    right_send, left_send, left_recv, right_recv, on_send, on_recv, sib_send, sib_recv,
    abp_sem, abu_send, abu_recv, abd_send, abd_recv,
    yx_send, yx_recv, own_send, own_recv, gos_sem,
):
    half = nz // 2
    jump = half // 2 if half >= 4 else 0
    firsts = (1, jump) if jump else (1,)
    width = hd // 4
    rows = hd // (2 * nz)
    heads = hd // HEAD
    scale = 1.0 / math.sqrt(hd * rank)

    gossip, zero = lax.axis_index("gossip"), lax.axis_index("zero")
    core = lax.rem(gossip, 2)
    y_lo = lax.rem(lax.div(gossip, 2), 2)
    x = lax.div(gossip, 4)
    z = lax.div(zero, 2)
    y_hi = lax.rem(zero, 2)
    y = y_hi * 2 + y_lo
    place = core * y + (1 - core) * x

    def spread_device(step):
        xs = lax.rem(x + step + RING, RING)
        ys = lax.rem(y + step + RING, RING)
        g0, z0 = (xs * 2 + y_lo) * 2, zero
        g1, z1 = (x * 2 + lax.rem(ys, 2)) * 2 + 1, z * 2 + lax.div(ys, 2)
        return core * g1 + (1 - core) * g0, core * z1 + (1 - core) * z0

    def z_device(step):
        return gossip, lax.rem(z + step + nz, nz) * 2 + y_hi

    opposite = ((x * 2 + 1 - y_lo) * 2 + core, z * 2 + 1 - y_hi)
    sibling = ((x * 2 + y_lo) * 2 + 1 - core, zero)
    mate = (gossip, z * 2 + 1 - y_hi)
    right, left = spread_device(1), spread_device(-1)
    after = (lax.rem(gossip + DIST, n_gossip), zero)
    before = (lax.rem(gossip + n_gossip - DIST, n_gossip), zero)

    barrier = pltpu.get_barrier_semaphore()

    def greet(device):
        pl.semaphore_signal(barrier, inc=1, device_id=device, device_id_type=MESH)

    partners = [right, left, opposite, sibling, mate, after, before]
    for s in firsts:
        partners += [z_device(s), z_device(-s)] if 2 * s != nz else [z_device(s)]
    for device in partners:
        greet(device)

    def block(step):
        p = lax.rem(place + step + RING, RING)
        return core * 2 + lax.rem(p, 2), lax.div(p, 2)

    kb, r = block(0)
    crosses = (r == y_hi) & (core == 0)

    def plane(i):
        s, odd = lax.div(i + 1, 2), lax.rem(i, 2)
        return lax.rem(z + nz + s - 2 * odd * s, nz)

    def copy(src, dst, send, recv, device):
        return pltpu.make_async_remote_copy(
            src_ref=src, dst_ref=dst, send_sem=send, recv_sem=recv, device_id=device, device_id_type=MESH
        )

    loads = [
        pltpu.make_async_copy(q_hbm.at[0], q, load_sem.at[1]),
        pltpu.make_async_copy(k_hbm.at[0], k, load_sem.at[2]),
        pltpu.make_async_copy(v_hbm.at[0], v, load_sem.at[3]),
    ]
    own = pltpu.make_async_copy(
        w_hbm.at[:, pl.ds(pl.multiple_of(kb * width, 128), width)], wt.at[kb, z, r], load_sem.at[0]
    )

    @pl.when(r == y_hi)
    def _():
        own.start()

    small = [
        pltpu.make_async_copy(a_hbm.at[0], factors_in.at[0], load_sem.at[4]),
        pltpu.make_async_copy(b_hbm.at[0], factors_in.at[1], load_sem.at[5]),
        pltpu.make_async_copy(pattern_hbm, pattern, load_sem.at[6]),
    ]
    for load in [*small, *loads]:
        load.start()

    square[...] = jnp.zeros_like(square)
    for load in small:
        load.wait()
    square[0:rank, 0:rows] = factors_in[0]
    square[rank:, 0:rows] = factors_in[1]
    abf[...] = square[...].T[0:rows]
    ab[z, y_hi] = abf[...].astype(BF16)

    key_at = lax.broadcasted_iota(jnp.int32, (TILE, 2 * TILE), 0)
    query_at = lax.broadcasted_iota(jnp.int32, (TILE, 2 * TILE), 1)
    sees = (pattern[0, 1, 1] == 0) | (pattern[0, 1, 2] == 0)
    far = jnp.where(sees, F32(0.0), F32(-1e30))
    mask0[...] = jnp.where(query_at < TILE, jnp.where(key_at <= query_at, F32(0.0), F32(-1e30)), far)
    mask1[...] = jnp.where(key_at <= query_at, F32(0.0), F32(-1e30))[:, 0:TILE]

    @pl.when(r == y_hi)
    def _():
        own.wait()

    pl.semaphore_wait(barrier, len(partners))

    def cross():
        return copy(wt.at[kb, z, r], wt.at[kb, z, r], opp_sem.at[0], opp_sem.at[1], opposite)

    middle = (rows // 2 + 15) // 16 * 16
    parts = ((0, middle), (middle, rows - middle))

    def up(s, slot, n):
        at = wt.at[kb, lax.rem(z - s + nz, nz), r, pl.ds(*parts[n])]
        return copy(at, at, zu_send.at[slot, n], zu_recv.at[slot, n], z_device(1))

    def down(s, slot, n):
        at = wt.at[kb, lax.rem(z + s, nz), r, pl.ds(*parts[n])]
        return copy(at, at, zd_send.at[slot, n], zd_recv.at[slot, n], z_device(-1))

    def to_right(i):
        at = wt.at[kb, plane(i), r]
        return copy(at, at, right_send.at[i], left_recv.at[i], right)

    def to_left(i):
        at = wt.at[kb, plane(i), r]
        return copy(at, at, left_send.at[i], right_recv.at[i], left)

    def from_left(i):
        n, m = block(-1)
        at = wt.at[n, plane(i), m]
        return copy(at, at, on_send.at[i], left_recv.at[i], right)

    def from_right(i):
        n, m = block(1)
        at = wt.at[n, plane(i), m]
        return copy(at, at, on_send.at[i], right_recv.at[i], left)

    def on_right(i):
        n, m = block(-1)
        at = wt.at[n, plane(i), m]
        return copy(at, at, on_send.at[i], on_recv.at[i], right)

    def on_left(i):
        n, m = block(1)
        at = wt.at[n, plane(i), m]
        return copy(at, at, on_send.at[i], on_recv.at[i], left)

    def on_in(i):
        n, m = block(2)
        at = wt.at[n, plane(i), m]
        return copy(at, at, on_send.at[i], on_recv.at[i], right)

    def across(i):
        at = wt.at[pl.ds(core * 2, 2), plane(i)]
        return copy(at, at, sib_send.at[i], sib_recv.at[i], sibling)

    def across_in(i):
        at = wt.at[pl.ds(2 - core * 2, 2), plane(i)]
        return copy(at, at, sib_send.at[i], sib_recv.at[i], sibling)

    def spread(i):
        to_right(i).start()
        to_left(i).start()

    def arrive(s):
        for n in range(2):
            if s < half or n == 0:
                up(s, s, n).wait_recv()
            if s < half - 1 or (s < half and n == 0):
                up(s, s + 1, n).start()
            if s < half or n == 1:
                down(s, s, n).wait_recv()
            if s < half - 1 or (s < half and n == 1):
                down(s, s + 1, n).start()
        spread(2 * s - 1)
        if s < half:
            spread(2 * s)

    def hand_on(s):
        i = max(2 * s - 1, 0)
        from_left(i).wait_recv()
        on_right(i).start()
        from_right(i).wait_recv()
        if 0 < s < half:
            from_right(2 * s).wait_recv()
            on_left(2 * s).start()
            from_left(2 * s).wait_recv()

    def share(s):
        on_in(max(2 * s - 1, 0)).wait_recv()
        across(max(2 * s - 1, 0)).start()
        if 0 < s < half:
            on_in(2 * s).wait_recv()
            across(2 * s).start()

    def ab_mate(which):
        at = ab.at[z, which]
        return copy(at, at, abp_sem.at[0], abp_sem.at[1], mate)

    def ab_up(s, step=1):
        at = ab.at[lax.rem(z - s + nz, nz)]
        return copy(at, at, abu_send.at[s + step], abu_recv.at[s + step], z_device(step))

    def ab_down(s, step=1):
        at = ab.at[lax.rem(z + s, nz)]
        return copy(at, at, abd_send.at[s + step], abd_recv.at[s + step], z_device(-step))

    def ab_in(s):
        at = ab.at[lax.rem(z - s + nz, nz)]
        copy(at, at, abu_send.at[s], abu_recv.at[s], z_device(1)).wait_recv()
        if s < half and s + 1 not in firsts:
            ab_up(s).start()
        if s < half:
            at = ab.at[lax.rem(z + s, nz)]
            copy(at, at, abd_send.at[s], abd_recv.at[s], z_device(-1)).wait_recv()
            if s < half - 1 and s + 1 not in firsts:
                ab_down(s).start()

    fold = F32(math.log2(math.e) / math.sqrt(HEAD))

    def attend(first, last):
        @pl.loop(first, last)
        def _(h):
            at = pl.ds(pl.multiple_of(h * HEAD, HEAD), HEAD)
            qh = q[:, at]
            s0 = nt(k[0:TILE, at], qh) * fold + mask0[...]
            s1 = nt(k[TILE:, at], qh[TILE:]) * fold + mask1[...]
            top0 = jnp.max(s0, axis=0, keepdims=True)
            top1 = jnp.max(s1, axis=0, keepdims=True)
            top1 = jnp.maximum(top0[:, TILE:], top1)
            e00 = jnp.exp2(s0[:, 0:TILE] - top0[:, 0:TILE])
            e01 = jnp.exp2(s0[:, TILE:] - top1)
            e11 = jnp.exp2(s1 - top1)
            total0 = jnp.sum(e00, axis=0, keepdims=True)
            total1 = jnp.sum(e01, axis=0, keepdims=True) + jnp.sum(e11, axis=0, keepdims=True)
            part0, part1 = 1.0 / total0, 1.0 / total1
            v0, v1 = v[0:TILE, at], v[TILE:, at]
            c0 = tn(v0, (e00 * part0).astype(BF16))
            c1 = tn(v0, (e01 * part1).astype(BF16)) + tn(v1, (e11 * part1).astype(BF16))
            ctx[at, 0:TILE] = c0.astype(BF16)
            ctx[at, TILE:] = c1.astype(BF16)

    def sides(part):
        nothing = jnp.zeros((2 * rank, 2 * TILE), F32)
        return jnp.concatenate([part, nothing, part], axis=0).T.astype(BF16)

    def adapt():
        both = tn(ab[...].reshape(hd, 2 * rank), ctx[...])
        low[0:rank] = jnp.zeros((rank, 2 * TILE), BF16)
        low[rank:] = both[0:rank].astype(BF16)
        low_t[...] = sides(low[rank:].astype(F32))

    def pack(g, w, wide):
        for m in range(2):
            lower = wide[m * rows + middle : (m + 1) * rows, 2 * rank :]
            if 2 * middle > rows:
                lower = jnp.concatenate([lower, jnp.zeros((2 * middle - rows, 2 * rank), F32)], axis=0)
            grads[g, w, m] = (scale * (wide[m * rows : m * rows + middle, 0 : 2 * rank] + lower)).astype(BF16)

    def trade(g, i):
        w = plane(i)
        return copy(grads.at[g, w, 1 - y_hi], theirs.at[g, w], yx_send.at[g, i], yx_recv.at[g, i], mate)

    def give(g, i):
        w = plane(i)
        owner = (gossip, w * 2 + y_hi)
        return copy(summed.at[g, w], landed.at[g, z], own_send.at[g, i], own_recv.at[g, z], owner)

    def take(g, i):
        w = plane(i)
        owner = (gossip, w * 2 + y_hi)
        return copy(summed.at[g, w], landed.at[g, w], own_send.at[g, i], own_recv.at[g, w], owner)

    def pass_on(g, i):
        w = plane(i)
        trade(g, i).wait_recv()
        summed[g, w] = (grads[g, w, y_hi].astype(F32) + theirs[g, w].astype(F32)).astype(BF16)
        give(g, i).start()

    def collect(g):
        trade(g, 0).wait_recv()
        total[g] = grads[g, z, y_hi].astype(F32) + theirs[g, z].astype(F32)

        @pl.loop(1, nz)
        def _(i):
            take(g, i).wait_recv()
            total[g] += landed[g, plane(i)].astype(F32)

    based = []

    def product(planes):
        weights = [jnp.concatenate([wt[n, w].reshape(2 * rows, width) for w in planes], axis=0) for n in range(4)]
        return nn(jnp.concatenate(weights, axis=1), ctx[...])

    def prepare(s):
        members = [max(2 * s - 1, 0)] + ([2 * s] if 0 < s < half else [])
        for i in members:
            across_in(i).wait_recv()
        planes = [plane(i) for i in members]
        out = product(planes)
        for n, w in enumerate(planes):
            base[w] = out[n * 2 * rows : (n + 1) * 2 * rows]
        based.append(s)

    def project(s):
        members = [max(2 * s - 1, 0)] + ([2 * s] if 0 < s < half else [])
        if s not in based:
            for i in members:
                across_in(i).wait_recv()
        planes = [plane(i) for i in members]

        def rows_of(blocks):
            return jnp.concatenate([b.reshape(2 * rows, b.shape[-1]) for b in blocks], axis=0)

        factors = rows_of([ab[w] for w in planes])
        out = scale * nn(factors, low[...])
        if s in based:
            out += rows_of([base[w] for w in planes])
        else:
            out += product(planes)
        slope = jnp.tanh(SHARPNESS * out).astype(BF16)
        hid[...] += tn(factors, slope)
        wide = nn(slope, low_t[...])
        for n, w in enumerate(planes):
            pack(0, w, wide[n * 2 * rows : (n + 1) * 2 * rows])
            trade(0, members[n]).start()

    @pl.when(crosses)
    def _():
        cross().start()

    ab_mate(y_hi).start()

    @pl.when(r != y_hi)
    def _():
        cross().wait_recv()

    for n in range(2):
        up(0, 1, n).start()
        down(0, 1, n).start()
    spread(0)
    for load in loads:
        load.wait()
    hid[...] = jnp.zeros_like(hid)
    cut = [heads * n // 5 for n in range(6)]
    attend(cut[0], cut[1])
    ab_mate(1 - y_hi).wait_recv()
    for s in reversed(firsts):
        ab_up(0, s).start()
        if s < half:
            ab_down(0, s).start()
    attend(cut[1], cut[2])
    chains = [range(a, b) for a, b in zip(firsts, (*firsts[1:], half + 1))]
    ticks = [[s for s in tick if s is not None] for tick in itertools.zip_longest(*chains)]
    todo, traded = [], []

    def work_off(count):
        for s in todo[:count]:
            project(s)
            traded.append([i for i in ((2 * s - 1, 2 * s) if s < half else (2 * s - 1,)) if i > 0])
        del todo[:count]

    def pass_off(count):
        for group in traded[:count]:
            for i in group:
                pass_on(0, i)
        del traded[:count]

    for t in range(1, half + 1):
        arrive(t)
        if t <= len(ticks):
            for s in ticks[t - 1]:
                ab_in(s)
        if t <= 3:
            attend(cut[t + 1], cut[t + 2])
        if t == len(ticks):
            adapt()
        hand_on(t - 1)
        if t >= 2:
            share(t - 2)
            todo.append(t - 2)
        if 3 <= t < half:
            prepare(t - 3)
        if t > len(ticks):
            work_off(PLAN[t - len(ticks) - 1][0])
            pass_off(PLAN[t - len(ticks) - 1][1])
    for t in range(half, 3):
        attend(cut[t + 2], cut[t + 3])
    hand_on(half)
    share(half - 1)
    todo.append(half - 1)
    pass_off(1)
    work_off(len(todo) - 1)
    pass_off(1)
    share(half)
    todo.append(half)
    work_off(1)
    pass_off(2)
    work_off(len(todo))

    hid_t = sides(hid[rank:])

    def send_a(n):
        i = nz - 1 - n
        w = plane(i)
        part = ctx[pl.ds(pl.multiple_of(w * 2 * rows, 2 * rows), 2 * rows)]
        pack(1, w, nn(part, hid_t))
        trade(1, i).start()

    pl.loop(0, half)(send_a)
    pass_off(len(traded))
    pl.loop(half, nz)(send_a)

    @pl.loop(0, nz - 1)
    def _(n):
        pass_on(1, nz - 1 - n)

    collect(0)
    collect(1)

    def unpack(g, turn):
        straight, turned = total[g], pltpu.roll(total[g], rank, 1)
        if turn:
            straight, turned = turned, straight
        return jnp.concatenate([straight, turned[0 : rows - middle]], axis=0)

    column = lax.broadcasted_iota(jnp.int32, (rows, 2 * rank), 1)
    gradient = jnp.where(column < rank, unpack(1, False), unpack(0, True))
    moved[...] = abf[...] - STEP_RATE * gradient
    gossip_copy = copy(moved, partner, gos_sem.at[0], gos_sem.at[1], after)
    gossip_copy.start()

    @pl.when(crosses)
    def _():
        cross().wait_send()

    ab_mate(y_hi).wait_send()

    up(half - 1, half, 0).wait_send()
    down(half - 1, half, 1).wait_send()

    @pl.loop(0, half)
    def _(s):
        ab_up(s).wait_send()

    @pl.loop(0, half - 1)
    def _(s):
        for n in range(2):
            up(s, s + 1, n).wait_send()
            down(s, s + 1, n).wait_send()
        ab_down(s).wait_send()

    @pl.loop(0, nz)
    def _(i):
        to_right(i).wait_send()
        to_left(i).wait_send()
        on_in(i).wait_send()
        across(i).wait_send()
        trade(0, i).wait_send()
        trade(1, i).wait_send()

    @pl.loop(1, nz)
    def _(i):
        give(0, i).wait_send()
        give(1, i).wait_send()

    gossip_copy.wait_recv()
    new = 0.5 * (moved[...] + partner[...])
    square[...] = jnp.zeros_like(square)
    square[0:rows] = new
    turned = square[...].T
    out[...] = turned[:, 0:rows]
    gossip_copy.wait_send()


def part_in_two(rank, both, upper, lower):
    upper[0] = both[0:rank]
    lower[0] = both[rank:]


def solution(mesh):
    n_gossip, n_zero = mesh.shape["gossip"], mesh.shape["zero"]
    nz = n_zero // 2
    half = nz // 2

    def per_device(queries, keys, values, pattern, out_weight, adapt_a, adapt_b):
        _, tokens, hd = queries.shape
        rows, rank = adapt_a.shape[1:]
        width = hd // 4
        middle = (rows // 2 + 15) // 16 * 16
        dma = pltpu.SemaphoreType.DMA
        vmem = pltpu.VMEM
        whole = pl.BlockSpec(memory_space=pltpu.VMEM)
        place = pl.BlockSpec(memory_space=pl.ANY)
        flops = 2 * tokens * hd * (hd + 2 * tokens + 4 * rank)
        new = pl.pallas_call(
            functools.partial(kernel, nz, n_gossip, hd, rank),
            out_shape=jax.ShapeDtypeStruct((2 * rank, rows), F32),
            in_specs=[place] * 7,
            out_specs=whole,
            scratch_shapes=[
                vmem((tokens, hd), BF16), vmem((tokens, hd), BF16), vmem((tokens, hd), BF16),
                pltpu.SMEM(pattern.shape, jnp.int32), vmem((2, rank, rows), F32),
                vmem((4, nz, 2, rows, width), BF16),
                vmem((nz, 2, rows, 2 * rank), BF16), vmem((rows, 2 * rank), F32), vmem((2 * rank, 128), F32),
                vmem((TILE, 2 * TILE), F32), vmem((TILE, TILE), F32),
                vmem((hd, tokens), BF16), vmem((2 * rank, tokens), BF16), vmem((tokens, 4 * rank), BF16),
                vmem((nz, 2 * rows, tokens), F32), vmem((2 * rank, tokens), F32), vmem((2, nz, 2, middle, 2 * rank), BF16),
                vmem((2, nz, middle, 2 * rank), BF16), vmem((2, nz, middle, 2 * rank), BF16),
                vmem((2, nz, middle, 2 * rank), BF16), vmem((2, middle, 2 * rank), F32),
                vmem((rows, 2 * rank), F32), vmem((rows, 2 * rank), F32),
                dma((7,)), dma((2,)),
                dma((half + 1, 2)), dma((half + 1, 2)), dma((half + 1, 2)), dma((half + 1, 2)),
                dma((nz,)), dma((nz,)), dma((nz,)), dma((nz,)), dma((nz,)), dma((nz,)), dma((nz,)), dma((nz,)),
                dma((2,)), dma((half + 1,)), dma((half + 1,)), dma((half + 1,)), dma((half + 1,)),
                dma((2, nz)), dma((2, nz)), dma((2, nz)), dma((2, nz)), dma((2,)),
            ],
            compiler_params=pltpu.CompilerParams(
                collective_id=0, has_side_effects=True, vmem_limit_bytes=60 * 1024 * 1024
            ),
            cost_estimate=pl.CostEstimate(flops=flops, bytes_accessed=8 * tokens * hd, transcendentals=tokens * hd),
        )(queries, keys, values, pattern, out_weight.T, adapt_a.transpose(0, 2, 1), adapt_b)
        half_shape = jax.ShapeDtypeStruct((1, rank, rows), F32)
        new_a, new_b = pl.pallas_call(
            functools.partial(part_in_two, rank), out_shape=(half_shape, half_shape), in_specs=[whole], out_specs=(whole, whole)
        )(new)
        return new_a.transpose(0, 2, 1), new_b

    placed = (
        P(("gossip", "zero"), None, None),
        P(("gossip", "zero"), None, None),
        P(("gossip", "zero"), None, None),
        P(("gossip", "zero"), None, None),
        P(None, "zero"),
        P("gossip", "zero", None),
        P("gossip", None, "zero"),
    )
    return jax.shard_map(
        per_device,
        mesh=mesh,
        in_specs=placed,
        out_specs=(P("gossip", "zero", None), P("gossip", None, "zero")),
        check_vma=False,
    )
```
